256 devices in a mesh: section: 2 (over core), row: 8 (over z), col: 16 (over x, y).
Axes of the slice: x: 4, y: 4, z: 8, core: 2. Of those that a mesh axis runs over, the one named last changes fastest.
Arguments:
- tokens: bfloat16 [2048, 8192], P('row', 'col'), may hold values from -6 to 6
- norm_gain: bfloat16 [2, 8192], P('section', 'col'), may hold values from 0.099609375 to 1.8984375
- w_query: bfloat16 [2, 8192, 4096], P('section', 'row', 'col'), may hold values from -0.75 to 0.75
- w_keyval: bfloat16 [2, 8192, 2048], P('section', 'row', 'col'), may hold values from -0.75 to 0.75, as said below
- w_out: bfloat16 [2, 4096, 8192], P('section', 'row', 'col'), may hold values from -0.09375 to 0.09375
- subtree_last: int32 [2048], P('row'), may hold values from 0 to 255, as said below
- block_live: int32 [8, 2, 2], P('row'), may hold values from 0 to 1, as said below
Outputs:
- after_section: bfloat16 [2, 2048, 8192], P('section', 'row', 'col')
The draws below stay inside these ranges and needn't reach their ends.
Inputs may be any that keep to these rules, and one draw needn't show every extreme that they name: Each tree's tokens are in preorder: local index 0 is the root, and subtree_last[t] is the local index of the last token in t's subtree, so j is an ancestor of i or i itself exactly when j <= i <= subtree_last[j]. block_live[t, b, b] = 1 and block_live[t, b, c] = 0 for c > b. `w_keyval`: weights of order D ** -0.5.
All inputs are finite; a program needn't handle non-finite values.
Results may differ from the reference program's by a relative error of at most 0.008.
Values may be sent and summed in bfloat16 or wider, within the bound.
A program may use at most 64 MiB of HBM per device.

```python
import jax
import jax.numpy as jnp
from jax import lax

D = 8192
H = 32
KV = 8
DH = 128
BLOCK = 128
TREE = 256
TREES = 8
TOKENS = 2048
MICRO = 2


def key_base(key):
    return jax.random.normal(key, (2, D, KV, DH), jnp.float32)


def draw_w_keyval(key, part):
    shared = key_base(key)
    key = jax.random.fold_in(key, 11)
    values = jax.random.normal(key, (2, D, KV, DH), jnp.float32)
    stacked = jnp.stack([shared, values], axis=3).reshape(2, D, 2 * KV * DH)
    return jnp.clip(stacked * D ** (-0.5), -0.75, 0.75).astype(jnp.bfloat16)


def draw_w_query(key, part):
    key = jax.random.fold_in(key, 12)
    noise = jax.random.normal(key, (2, D, H, DH), jnp.float32)
    mixed = noise
    return jnp.clip(mixed.reshape(2, D, H * DH) * D ** (-0.5), -0.75, 0.75).astype(jnp.bfloat16)


def draw_subtree_last(key, part):
    key = jax.random.fold_in(key, 21)
    first_key, second_key = jax.random.split(key)
    deeper = jax.random.randint(first_key, (TREE - 1, TREES), 0, 4)
    jumps = jax.random.randint(second_key, (TREE - 1, TREES), 0, 1 << 20)

    def advance(depth, inputs):
        step_kind, jump = inputs
        upward = 1 + jump % jnp.maximum(depth, 1)
        new_depth = jnp.where(step_kind > 0, depth + 1, upward)
        return (new_depth, new_depth)
    start = jnp.zeros((TREES,), jnp.int32)
    unused, depths = lax.scan(advance, start, (deeper, jumps))
    depths = jnp.concatenate([start[None, :], depths], axis=0).T
    positions = jnp.arange(TREE, dtype=jnp.int32)
    later = positions[None, :] > positions[:, None]
    stops = later[None] & (depths[:, None, :] <= depths[:, :, None])
    first_stop = jnp.min(jnp.where(stops, positions[None, None, :], TREE), axis=2)
    return (first_stop - 1).astype(jnp.int32).reshape(TREES * TREE)


def draw_block_live(key, part):
    key = jax.random.fold_in(key, 31)
    coins = jax.random.randint(key, (TREES, MICRO, MICRO), 0, 3)
    query_block = jnp.arange(MICRO, dtype=jnp.int32)[:, None]
    key_block = jnp.arange(MICRO, dtype=jnp.int32)[None, :]
    below = jnp.where(coins > 0, 1, 0)
    table = jnp.where(key_block < query_block, below, jnp.where(key_block == query_block, 1, 0))
    return jnp.broadcast_to(table, (TREES, MICRO, MICRO)).astype(jnp.int32)


def block_levels(key, extent, cuts, least, top_value):
    loudness = 1.0
    for position, shards_of in cuts:
        steps = jax.random.uniform(jax.random.fold_in(jax.random.fold_in(key, 6), position), (shards_of,), jnp.float32, least / len(cuts), top_value / len(cuts))
        loudness = loudness * jnp.repeat(jnp.exp(steps), extent[position] // shards_of).reshape((-1,) + (1,) * (len(extent) - 1 - position))
    return loudness


def centred(key, shape, scale, most, pieces=(), kind=jnp.bfloat16):
    array = scale * jax.random.normal(key, shape, jnp.float32)
    if pieces:
        array = array * block_levels(key, shape, pieces, -0.22, 0.18)
    return jnp.clip(array, -most, most).astype(kind)


def setup_inputs(seed: int = 0) -> dict:
    key_of = jax.random.split(jax.random.key(seed), 8)
    tokens = centred(key_of[0], (TOKENS, D), 1.0, 6.0, ((0, 8), (1, 16)))
    norm_gain = jnp.clip(1.0 + 0.18 * jax.random.normal(key_of[1], (2, D), jnp.float32), 0.099609375, 1.8984375).astype(jnp.bfloat16)
    w_query = draw_w_query(jax.random.fold_in(key_of[7], 71), 0)
    w_keyval = draw_w_keyval(jax.random.fold_in(key_of[7], 71), 0)
    w_out = centred(key_of[4], (2, H * DH, D), (H * DH) ** -0.5, 0.09375, ((0, 2), (1, 8), (2, 16)))
    subtree_last = draw_subtree_last(jax.random.fold_in(key_of[7], 71), 0)
    block_live = draw_block_live(jax.random.fold_in(key_of[7], 71), 0)
    return {"tokens": tokens, "norm_gain": norm_gain, "w_query": w_query, "w_keyval": w_keyval, "w_out": w_out, "subtree_last": subtree_last, "block_live": block_live}


EPSILON = 1e-05

def build_mask(subtree_end, live_table):
    positions = jnp.arange(TREE, dtype=jnp.int32)
    block_of = positions // BLOCK
    allowed = (positions[None, :] <= positions[:, None]) & (positions[:, None] <= subtree_end[None, :])
    picked = live_table[block_of[:, None], block_of[None, :]] > 0
    return allowed & picked

def one_layer(hidden, gains, w_q, w_kv, w_o, subtree_last, block_live):
    wide_float = hidden.astype(jnp.float32)
    inverse_rms = lax.rsqrt(lax.optimization_barrier(jnp.mean(wide_float * wide_float, axis=1, keepdims=True)) + EPSILON)
    normed = (wide_float * inverse_rms * gains.astype(jnp.float32)).astype(jnp.bfloat16)
    query = jnp.dot(normed, w_q, preferred_element_type=jnp.float32).astype(jnp.bfloat16)
    key_value = jnp.dot(normed, w_kv, preferred_element_type=jnp.float32).astype(jnp.bfloat16)
    group_size = H // KV
    query = query.reshape(TREES, TREE, KV, group_size, DH)
    key_value = key_value.reshape(TREES, TREE, KV, 2, DH)

    def one_tree(inputs):
        tree_query, tree_kv, subtree_end, live_table = inputs
        allowed = build_mask(subtree_end, live_table)
        scores = jnp.einsum('qkgd,skd->kgqs', tree_query.astype(jnp.float32), tree_kv[:, :, 0].astype(jnp.float32)) * DH ** (-0.5)
        scores = jnp.where(allowed[None, None], scores, jnp.float32(-1e+30))
        row_max = lax.optimization_barrier(jnp.max(scores, axis=3, keepdims=True))
        raw_weights = jnp.exp(scores - row_max)
        probs = (raw_weights / lax.optimization_barrier(jnp.sum(raw_weights, axis=3, keepdims=True))).astype(jnp.bfloat16)
        mixed = jnp.einsum('kgqs,skd->qkgd', probs.astype(jnp.float32), tree_kv[:, :, 1].astype(jnp.float32))
        return mixed.astype(jnp.bfloat16).reshape(TREE, H * DH)
    attended = lax.map(one_tree, (query, key_value, subtree_last.reshape(TREES, TREE), block_live))
    attended = attended.reshape(TREES * TREE, H * DH)
    projected = jnp.dot(attended, w_o, preferred_element_type=jnp.float32)
    return (wide_float + projected).astype(jnp.bfloat16)

def reference(tokens, norm_gain, w_query, w_keyval, w_out, subtree_last, block_live):
    first = one_layer(tokens, norm_gain[0], w_query[0], w_keyval[0], w_out[0], subtree_last, block_live)
    second = one_layer(first, norm_gain[1], w_query[1], w_keyval[1], w_out[1], subtree_last, block_live)
    return jnp.stack([first, second])
```

```python
import jax
import jax.numpy as jnp
from jax import lax
from jax.experimental import pallas as pl
from jax.experimental.pallas import tpu as pltpu
from jax.sharding import PartitionSpec as P

MESH = pl.DeviceIdType.MESH
D = 8192
DH = 128
BLOCK = 128
TREE = 256
ROWS = 8
COLS = 16
SIDE = 4
HALF = 256
STAT = 16
EPSILON = 1e-05
BF = jnp.bfloat16
F32 = jnp.float32


def kernel(
    tok_ref, gain_ref, wq_ref, wkv_ref, wo_ref, last_ref, live_ref, out_ref,
    w_in, w_out, xbuf, mbuf, gains, acc, acc_o, ex_q, ex_kv, ex_pair, kv_bf, stat, ex_stat,
    ex_o, ex_last, x1buf,
    wi_send, wi_recv, wo_send, wo_recv, own_send, own_sem, gain_send, gain_recv,
    x_send, x_recv, m_send, m_recv, ex_send, ex_recv, pair_send, pair_recv,
    o_send, o_recv, last_send, last_recv, x1_send, x1_recv,
):
    sec = lax.axis_index("section")
    row = lax.axis_index("row")
    col = lax.axis_index("col")
    other = 1 - sec
    cx, cy = col // SIDE, lax.rem(col, SIDE)
    partner = jnp.where(lax.rem(col, 2) == 1, col - 1, col + 1)
    sibling = (other, row, col)
    ends = []

    def peer(j):
        return lax.rem(cx + j // SIDE, SIDE) * SIDE + lax.rem(cy + lax.rem(j, SIDE), SIDE)

    def remote(src, dst, send, recv, device):
        return pltpu.make_async_remote_copy(
            src_ref=src, dst_ref=dst, send_sem=send, recv_sem=recv, device_id=device, device_id_type=MESH
        )

    barrier = pltpu.get_barrier_semaphore()
    up = (sec, lax.rem(row + 1, ROWS), col)
    down = (sec, lax.rem(row + ROWS - 1, ROWS), col)
    greeted = [sibling, up, down, (other, row, partner)]
    for device in greeted:
        pl.semaphore_signal(barrier, 1, device_id=device, device_id_type=MESH)

    def greet(j, carry):
        pl.semaphore_signal(barrier, 1, device_id=(sec, row, peer(j)), device_id_type=MESH)
        return carry

    lax.fori_loop(1, COLS, greet, 0)
    pl.semaphore_wait(barrier, len(greeted) + COLS - 1)

    gains[sec] = jnp.broadcast_to(gain_ref[...].astype(F32), (8, 2 * HALF))
    gain_copy = remote(gains.at[sec], gains.at[sec], gain_send, gain_recv, sibling)
    gain_copy.start()

    def own_parts(half, kind):
        parts = []
        for i in range(2):
            slot = 2 * row + i
            if kind == 0:
                base = pl.multiple_of(i * 512 + half * HALF, HALF)
                parts.append((wq_ref.at[pl.ds(base, HALF)], w_in.at[sec, slot, :, pl.ds(0, 256)]))
                parts.append((wkv_ref.at[pl.ds(base, HALF)], w_in.at[sec, slot, :, pl.ds(256, 128)]))
            else:
                base = pl.multiple_of(i * 256 + half * 128, 128)
                parts.append((wo_ref.at[pl.ds(base, 128)], w_out.at[sec, slot]))
        return parts

    swaps, keeps = [], []
    n = 0
    for kind in range(2):
        for (src, dst), (mine, place) in zip(own_parts(other, kind), own_parts(sec, kind)):
            swaps.append(remote(src, dst, own_send.at[n], own_sem.at[sec, n], sibling))
            keeps.append(pltpu.make_async_copy(mine, place, own_sem.at[sec, n]))
            n += 1
    for copy in keeps[:4] + keeps[4:]:
        copy.start()
    for copy in swaps:
        copy.start()

    def wait_own(s, kind):
        for n in range(4) if kind == 0 else range(4, 6):
            i = n // 2 if kind == 0 else n - 4
            slot = 2 * row + i
            if kind == 0:
                place = w_in.at[s, slot, :, pl.ds(0, 256) if n % 2 == 0 else pl.ds(256, 128)]
            else:
                place = w_out.at[s, slot]
            pltpu.make_async_copy(place, place, own_sem.at[s, n]).wait()

    def buffers(kind):
        return (w_in, wi_send, wi_recv) if kind == 0 else (w_out, wo_send, wo_recv)

    def forward(s, kind, d, way, i):
        buf, send, recv = buffers(kind)
        origin = lax.rem(row + (ROWS - d if way == 0 else d), ROWS)
        slot = 2 * origin + i
        place = buf.at[s, slot]
        copy = remote(place, place, send.at[s, way, 2 * d + i], recv.at[s, slot], up if way == 0 else down)
        copy.start()
        ends.append(copy)

    def arrived(s, kind, d, way, i):
        buf, send, recv = buffers(kind)
        origin = lax.rem(row + (ROWS - d if way == 0 else d), ROWS)
        slot = 2 * origin + i
        place = buf.at[s, slot]
        remote(place, place, send.at[s, way, 2 * d + i], recv.at[s, slot], sibling).wait_recv()

    def start_ring(s, kind):
        wait_own(s, kind)
        for i in range(2):
            for way in range(2):
                forward(s, kind, 0, way, i)

    def relay(s, kind, d):
        for i in range(2):
            for way in range(2):
                if d < 4 or i == way:
                    arrived(s, kind, d, way, i)
                    if d < 3 or (d == 3 and i == way):
                        forward(s, kind, d, way, i)

    def half_of(x):
        return jnp.where(sec == 0, x[:, :HALF], x[:, HALF:])

    def send_x(layer, x):
        gain = half_of(gains[layer])[0:1]
        xbuf[layer, col, :TREE] = (x * gain).astype(BF)
        square = x * x
        high = square.astype(BF)
        low = (square - high.astype(F32)).astype(BF)
        ones = jnp.ones((STAT, HALF), BF)
        dims = (((1,), (1,)), ((), ()))
        total = lax.dot_general(ones, high, dims, preferred_element_type=F32)
        total += lax.dot_general(ones, low, dims, preferred_element_type=F32)
        high = total.astype(BF).astype(F32)
        line = lax.broadcasted_iota(jnp.int32, (STAT, TREE), 0)
        rows = jnp.where(line == 0, high, jnp.where(line == 1, total - high, 0.0))
        xbuf[layer, col, TREE:] = rows.astype(BF)
        spread(xbuf, x_send, x_recv, layer)

    def spread(buf, send, recv, layer):
        def body(j, carry):
            block = buf.at[layer, col]
            remote(block, block, send.at[layer, j], recv.at[layer, col], (sec, row, peer(j))).start()
            return carry

        lax.fori_loop(1, COLS, body, 0)

    def spread_end(buf, send, recv, layer):
        def body(j, carry):
            block = buf.at[layer, col]
            remote(block, block, send.at[layer, j], recv.at[layer, col], (sec, row, peer(j))).wait_send()
            return carry

        lax.fori_loop(1, COLS, body, 0)

    def add_block(layer, c, first):
        @pl.when(c != col)
        def _():
            block = xbuf.at[layer, c]
            remote(block, block, x_send.at[layer, 0], x_recv.at[layer, c], sibling).wait_recv()

        part = jnp.dot(xbuf[layer, c, :TREE], w_in[layer, c], preferred_element_type=F32)
        lines = xbuf[layer, c, TREE:].astype(F32)
        if first:
            for g in range(3):
                acc[layer, g] = part[:, g * DH:(g + 1) * DH]
            stat[layer] = lines
        else:
            for g in range(3):
                acc[layer, g] += part[:, g * DH:(g + 1) * DH]
            stat[layer] += lines

    def exchange(layer):
        copies = [
            remote(acc.at[layer, other], ex_q.at[layer], ex_send.at[layer, 0], ex_recv.at[layer, 0], sibling),
            remote(acc.at[layer, 2], ex_kv.at[layer], ex_send.at[layer, 1], ex_recv.at[layer, 1], sibling),
            remote(stat.at[layer], ex_stat.at[layer], ex_send.at[layer, 2], ex_recv.at[layer, 2], sibling),
        ]
        kv_bf[layer] = acc[layer, 2].astype(BF)
        for k in range(2):
            copies.append(
                remote(
                    kv_bf.at[layer], ex_pair.at[layer, sec], pair_send.at[layer, k],
                    pair_recv.at[layer, sec], (k, row, partner),
                )
            )
        for copy in copies[3:] + copies[:3]:
            copy.start()
        ends.extend(copies)
        return copies

    def attend(layer, copies):
        for copy in copies[:3]:
            copy.wait_recv()
        lines = stat[layer] + ex_stat[layer]
        total = jnp.sum(lines, axis=0, keepdims=True)
        inverse = lax.rsqrt(total * (1.0 / D) + EPSILON)
        inverse = jnp.transpose(jnp.broadcast_to(inverse, (DH, TREE)))
        query = ((acc[layer, sec] + ex_q[layer]) * inverse).astype(BF)
        mine = ((acc[layer, 2] + ex_kv[layer]) * inverse).astype(BF)
        for k in range(2):
            place = ex_pair.at[layer, k]
            remote(place, place, pair_send.at[layer, k], pair_recv.at[layer, k], sibling).wait_recv()
        theirs = ((ex_pair[layer, 0].astype(F32) + ex_pair[layer, 1].astype(F32)) * inverse).astype(BF)
        odd = lax.rem(col, 2) == 1
        keys = jnp.where(odd, theirs, mine)
        values = jnp.where(odd, mine, theirs)
        scores = lax.dot_general(
            query, keys, (((1,), (1,)), ((), ())), preferred_element_type=F32
        ) * DH ** (-0.5)
        qpos = lax.broadcasted_iota(jnp.int32, (TREE, TREE), 0)
        kpos = lax.broadcasted_iota(jnp.int32, (TREE, TREE), 1)
        top, left = qpos < BLOCK, kpos < BLOCK
        live = jnp.where(
            top,
            jnp.where(left, live_ref[0, 0, 0], live_ref[0, 0, 1]),
            jnp.where(left, live_ref[0, 1, 0], live_ref[0, 1, 1]),
        )
        allowed = (kpos <= qpos) & (qpos <= last_ref[...]) & (live > 0)
        scores = jnp.where(allowed, scores, F32(-1e30))
        weights = jnp.exp(scores - jnp.max(scores, axis=1, keepdims=True))
        probs = (weights / jnp.sum(weights, axis=1, keepdims=True)).astype(BF)
        mbuf[layer, col] = jnp.dot(probs, values, preferred_element_type=F32).astype(BF)
        spread(mbuf, m_send, m_recv, layer)

    def project(layer):
        for h in range(2):
            acc_o[layer, h] = jnp.dot(
                mbuf[layer, col], w_out[layer, col, :, h * HALF:(h + 1) * HALF], preferred_element_type=F32
            )

        def body(j, carry):
            c = peer(j)
            block = mbuf.at[layer, c]
            remote(block, block, m_send.at[layer, 0], m_recv.at[layer, c], sibling).wait_recv()
            for h in range(2):
                acc_o[layer, h] += jnp.dot(
                    mbuf[layer, c], w_out[layer, c, :, h * HALF:(h + 1) * HALF], preferred_element_type=F32
                )
            return carry

        lax.fori_loop(1, COLS, body, 0)

    start_ring(0, 0)
    gain_copy.wait_send()
    remote(gains.at[other], gains.at[other], gain_send, gain_recv, sibling).wait_recv()
    x0 = half_of(tok_ref[...]).astype(F32)
    send_x(0, x0)
    add_block(0, 2 * row, True)
    add_block(0, 2 * row + 1, False)

    def add_ring(d):
        for way in range(2) if d < 4 else range(1):
            origin = lax.rem(row + (ROWS - d if way == 0 else d), ROWS)
            for i in range(2):
                add_block(0, 2 * origin + i, False)

    relay(0, 0, 1)
    add_ring(1)
    relay(0, 0, 2)
    start_ring(0, 1)
    add_ring(2)
    relay(0, 0, 3)
    relay(0, 1, 1)
    add_ring(3)
    relay(0, 0, 4)
    add_ring(4)
    copies = exchange(0)
    relay(0, 1, 2)
    start_ring(1, 0)
    attend(0, copies)
    relay(0, 1, 3)
    relay(1, 0, 1)
    relay(0, 1, 4)
    project(0)
    o_copy = remote(acc_o.at[0, other], ex_o, o_send, o_recv, sibling)
    o_copy.start()
    relay(1, 0, 2)
    start_ring(1, 1)
    o_copy.wait_recv()
    x1 = (half_of(tok_ref[...]).astype(F32) + (acc_o[0, sec] + ex_o[...])).astype(BF)
    x1buf[sec] = x1
    send_x(1, x1.astype(F32))
    x1_copy = remote(x1buf.at[sec], x1buf.at[sec], x1_send, x1_recv, sibling)
    x1_copy.start()
    relay(1, 0, 3)
    relay(1, 1, 1)
    remote(x1buf.at[other], x1buf.at[other], x1_send, x1_recv, sibling).wait_recv()

    @pl.when(sec == 0)
    def _():
        for h in range(2):
            out_ref[0, :, h * HALF:(h + 1) * HALF] = x1buf[h]

    relay(1, 0, 4)
    add_block(1, col, True)

    def add_peer(j, carry):
        add_block(1, peer(j), False)
        return carry

    lax.fori_loop(1, COLS, add_peer, 0)
    copies = exchange(1)
    relay(1, 1, 2)
    attend(1, copies)
    relay(1, 1, 3)
    relay(1, 1, 4)
    project(1)
    last_copy = remote(acc_o.at[1], ex_last, last_send, last_recv, (1, row, col))

    @pl.when(sec == 0)
    def _():
        last_copy.start()

    @pl.when(sec == 1)
    def _():
        last_copy.wait_recv()
        for h in range(2):
            x = x1buf[h].astype(F32)
            out_ref[0, :, h * HALF:(h + 1) * HALF] = (x + (acc_o[1, h] + ex_last[h])).astype(BF)

    for copy in swaps + ends + [o_copy, x1_copy]:
        copy.wait_send()
    for layer in range(2):
        spread_end(xbuf, x_send, x_recv, layer)
        spread_end(mbuf, m_send, m_recv, layer)

    @pl.when(sec == 0)
    def _():
        last_copy.wait_send()


def shards(tokens, norm_gain, w_query, w_keyval, w_out, subtree_last, block_live):
    vmem = pl.BlockSpec(memory_space=pltpu.VMEM)
    hbm = pl.BlockSpec(memory_space=pl.ANY)
    dma = pltpu.SemaphoreType.DMA
    return pl.pallas_call(
        kernel,
        out_shape=jax.ShapeDtypeStruct((1, TREE, 2 * HALF), BF),
        in_specs=[vmem, vmem, hbm, hbm, hbm, vmem, pl.BlockSpec(memory_space=pltpu.SMEM)],
        out_specs=vmem,
        scratch_shapes=[
            pltpu.VMEM((2, COLS, HALF, 3 * DH), BF),
            pltpu.VMEM((2, COLS, DH, 2 * HALF), BF),
            pltpu.VMEM((2, COLS, TREE + STAT, HALF), BF),
            pltpu.VMEM((2, COLS, TREE, DH), BF),
            pltpu.VMEM((2, 8, 2 * HALF), F32),
            pltpu.VMEM((2, 3, TREE, DH), F32),
            pltpu.VMEM((2, 2, TREE, HALF), F32),
            pltpu.VMEM((2, TREE, DH), F32),
            pltpu.VMEM((2, TREE, DH), F32),
            pltpu.VMEM((2, 2, TREE, DH), BF),
            pltpu.VMEM((2, TREE, DH), BF),
            pltpu.VMEM((2, STAT, TREE), F32),
            pltpu.VMEM((2, STAT, TREE), F32),
            pltpu.VMEM((TREE, HALF), F32),
            pltpu.VMEM((2, TREE, HALF), F32),
            pltpu.VMEM((2, TREE, HALF), BF),
            dma((2, 2, 8)), dma((2, COLS)), dma((2, 2, 8)), dma((2, COLS)),
            dma((6,)), dma((2, 6)), dma, dma,
            dma((2, COLS)), dma((2, COLS)), dma((2, COLS)), dma((2, COLS)),
            dma((2, 3)), dma((2, 3)), dma((2, 2)), dma((2, 2)),
            dma, dma, dma, dma, dma, dma,
        ],
        compiler_params=pltpu.CompilerParams(
            collective_id=0, has_side_effects=True, vmem_limit_bytes=40 << 20
        ),
    )(
        tokens, norm_gain, w_query[0], w_keyval[0], w_out[0],
        subtree_last.reshape(1, TREE), block_live,
    )


def solution(mesh):
    in_specs = (
        P("row", "col"),
        P("section", "col"),
        P("section", "row", "col"),
        P("section", "row", "col"),
        P("section", "row", "col"),
        P("row"),
        P("row", None, None),
    )
    out_specs = P("section", "row", "col")
    return jax.shard_map(shards, mesh=mesh, in_specs=in_specs, out_specs=out_specs, check_vma=False)
```

```python
import jax
import jax.numpy as jnp
from jax import lax
from jax.experimental import pallas as pl
from jax.experimental.pallas import tpu as pltpu
from jax.sharding import PartitionSpec as P

MESH = pl.DeviceIdType.MESH
D = 8192
DH = 128
BLOCK = 128
TREE = 256
ROWS = 8
COLS = 16
SIDE = 4
HALF = 256
STAT = 16
PARTS = 4
EPSILON = 1e-05
BF = jnp.bfloat16
F32 = jnp.float32


def kernel(
    tok_hbm, gain_ref, wq_ref, wkv_ref, wo_ref, last_ref, live_ref, out_ref,
    w_in, w_out, tok_ref, xbuf, mbuf, gains, acc, acc_o, ex_q, ex_kv, ex_pair, kv_bf, stat, ex_stat,
    ex_o, ex_last, x1buf, mask, tok_sem,
    wi_send, wi_recv, wo_send, wo_recv, own_send, own_sem, gain_send, gain_recv,
    x_send, x_recv, m_send, m_recv, ex_send, ex_recv, pair_send, pair_recv,
    o_send, o_recv, last_send, last_recv, x1_send, x1_recv,
):
    sec = lax.axis_index("section")
    row = lax.axis_index("row")
    col = lax.axis_index("col")
    other = 1 - sec
    cx, cy = col // SIDE, lax.rem(col, SIDE)
    odd = lax.rem(col, 2) == 1
    partner = jnp.where(odd, col - 1, col + 1)
    sibling = (other, row, col)
    up = (sec, lax.rem(row + 1, ROWS), col)
    down = (sec, lax.rem(row + ROWS - 1, ROWS), col)
    xs = [cx] + [lax.rem(cx + d, SIDE) for d in range(1, SIDE)]
    ys = [cy] + [lax.rem(cy + d, SIDE) for d in range(1, SIDE)]
    along_x = [(sec, row, x * SIDE + cy) for x in xs]
    along_y = [(sec, row, cx * SIDE + y) for y in ys]
    ends = []

    def remote(src, dst, send, recv, device):
        return pltpu.make_async_remote_copy(
            src_ref=src, dst_ref=dst, send_sem=send, recv_sem=recv, device_id=device, device_id_type=MESH
        )

    def launch(src, dst, send, recv, device):
        copy = remote(src, dst, send, recv, device)
        copy.start()
        ends.append(copy)
        return copy

    def landed(place, recv):
        remote(place, place, gain_send, recv, sibling).wait_recv()

    tok_copy = pltpu.make_async_copy(tok_hbm, tok_ref, tok_sem)
    tok_copy.start()
    barrier = pltpu.get_barrier_semaphore()
    greeted = [sibling, up, down, (other, row, partner)] + along_x[1:] + along_y[1:]
    for device in greeted:
        pl.semaphore_signal(barrier, 1, device_id=device, device_id_type=MESH)

    def slot_of(origin, i):
        return origin // 2, 2 * lax.rem(origin, 2) + i

    def own_parts(half, kind):
        parts = []
        for i in range(2):
            sx, sy = slot_of(row, i)
            if kind == 0:
                base = pl.multiple_of(i * 512 + half * HALF, HALF)
                parts.append((wq_ref.at[pl.ds(base, HALF)], w_in.at[sec, sx, sy, :, pl.ds(0, 256)]))
                parts.append((wkv_ref.at[pl.ds(base, HALF)], w_in.at[sec, sx, sy, :, pl.ds(256, 128)]))
            else:
                base = pl.multiple_of(i * 256 + half * 128, 128)
                parts.append((wo_ref.at[pl.ds(base, 128)], w_out.at[sec, sx, sy]))
        return parts

    swaps, keeps = [], []
    n = 0
    for kind in range(2):
        for (src, dst), (mine, place) in zip(own_parts(other, kind), own_parts(sec, kind)):
            swaps.append((src, dst, own_send.at[n], own_sem.at[sec, n], sibling))
            keeps.append(pltpu.make_async_copy(mine, place, own_sem.at[sec, n]))
            n += 1
    for copy in keeps:
        copy.start()
    gains[sec] = jnp.broadcast_to(gain_ref[...].astype(F32), (8, 2 * HALF))
    pl.semaphore_wait(barrier, len(greeted))
    for swap in swaps:
        launch(*swap)
    launch(gains.at[sec], gains.at[sec], gain_send, gain_recv, sibling)

    def wait_own(s, kind):
        for n in range(4) if kind == 0 else range(4, 6):
            sx, sy = slot_of(row, n // 2 if kind == 0 else n - 4)
            if kind == 0:
                place = w_in.at[s, sx, sy, :, pl.ds(0, 256) if n % 2 == 0 else pl.ds(256, 128)]
            else:
                place = w_out.at[s, sx, sy]
            pltpu.make_async_copy(place, place, own_sem.at[s, n]).wait()

    origins = {(0, 0): row, (0, 1): row}
    for d in range(1, 5):
        origins[d, 0] = lax.rem(row + ROWS - d, ROWS)
        origins[d, 1] = lax.rem(row + d, ROWS)

    def chunk(s, kind, d, way, i):
        buf, send, recv = (w_in, wi_send, wi_recv) if kind == 0 else (w_out, wo_send, wo_recv)
        sx, sy = slot_of(origins[d, way], i // 2)
        rows = (HALF if kind == 0 else DH) // 2
        place = buf.at[s, sx, sy, pl.ds(i % 2 * rows, rows)]
        return place, send.at[s, way, d, i], recv.at[s, sx, sy, i % 2]

    def forward(s, kind, d, way, i):
        place, send, recv = chunk(s, kind, d, way, i)
        launch(place, place, send, recv, up if way == 0 else down)

    def start_ring(s, kind):
        wait_own(s, kind)
        for i in range(PARTS):
            for way in range(2):
                forward(s, kind, 0, way, i)

    def relay(s, kind, d):
        for i in range(PARTS):
            for way in range(2):
                if d < 4 or i % 2 == way:
                    place, send, recv = chunk(s, kind, d, way, i)
                    landed(place, recv)
                    if d < 3 or (d == 3 and i % 2 == way):
                        forward(s, kind, d, way, i)

    def block_of(buf, recv, layer, h, along, across):
        x, y = (xs[across], ys[along]) if h == 0 else (xs[along], ys[across])
        return buf.at[layer, h, x, y], recv.at[layer, h, x, y]

    def phase_one(buf, send, recv, layer):
        for d in range(1, SIDE):
            for h in range(2):
                block, sem = block_of(buf, recv, layer, h, 0, 0)
                launch(block, block, send.at[layer, h, SIDE, d], sem, (along_y, along_x)[h][d])
        for d in range(1, SIDE):
            for h in range(2):
                block, sem = block_of(buf, recv, layer, h, 0, 0)
                launch(block, block, send.at[layer, h, 0, d], sem, (along_x, along_y)[h][d])

    def phase_two(buf, send, recv, layer):
        for j in (1, 3, 2):
            for h in range(2):
                block, sem = block_of(buf, recv, layer, h, j, 0)
                landed(block, sem)
                for d in range(1, SIDE):
                    launch(block, block, send.at[layer, h, j, d], sem, (along_x, along_y)[h][d])

    def group_landed(buf, recv, layer, h, d):
        for j in range(SIDE):
            landed(*block_of(buf, recv, layer, h, j, d))

    def half_of(x):
        return jnp.where(sec == 0, x[:, :HALF], x[:, HALF:])

    def prepare_x(layer, x):
        gain = half_of(gains[layer])[0:1]
        scaled = (x * gain).astype(BF)
        square = x * x
        high = square.astype(BF)
        low = (square - high.astype(F32)).astype(BF)
        ones = jnp.ones((STAT, DH), BF)
        dims = (((1,), (1,)), ((), ()))
        line = lax.broadcasted_iota(jnp.int32, (STAT, TREE), 0)
        for h in range(2):
            cols = slice(h * DH, (h + 1) * DH)
            total = lax.dot_general(ones, high[:, cols], dims, preferred_element_type=F32)
            total += lax.dot_general(ones, low[:, cols], dims, preferred_element_type=F32)
            top = total.astype(BF).astype(F32)
            rows = jnp.where(line == 0, top, jnp.where(line == 1, total - top, 0.0)).astype(BF)
            xbuf[layer, h, cx, cy, :TREE] = scaled[:, cols]
            for half in range(2):
                xbuf[layer, h, cx, cy, TREE + half * STAT:TREE + (half + 1) * STAT] = rows[:, half * DH:(half + 1) * DH]

    def add_stat(layer, blocks, first):
        lines = blocks[0][TREE:].astype(F32)
        for block in blocks[1:]:
            lines += block[TREE:].astype(F32)
        if first:
            stat[layer] = lines
        else:
            stat[layer] += lines

    def add_part(layer, part, first):
        for g in range(3):
            if first:
                acc[layer, g] = part[:, g * DH:(g + 1) * DH]
            else:
                acc[layer, g] += part[:, g * DH:(g + 1) * DH]

    def add_chunk(layer, d, way, i, first):
        sx, sy = slot_of(origins[d, way], i)
        blocks = [xbuf[layer, h, sx, sy] for h in range(2)]
        left = jnp.concatenate([block[:TREE] for block in blocks], axis=1)
        add_stat(layer, blocks, first)
        add_part(layer, jnp.dot(left, w_in[layer, sx, sy], preferred_element_type=F32), first)

    def add_group(layer, h, d, first):
        if h == 0:
            x = xs[d]
            blocks = [xbuf[layer, 0, x, y] for y in range(SIDE)]
            right = [w_in[layer, x, y, :DH] for y in range(SIDE)]
        else:
            y = ys[d]
            blocks = [xbuf[layer, 1, x, y] for x in range(SIDE)]
            right = [w_in[layer, x, y, DH:] for x in range(SIDE)]
        left = jnp.concatenate([block[:TREE] for block in blocks], axis=1)
        add_stat(layer, blocks, first)
        add_part(layer, jnp.dot(left, jnp.concatenate(right, axis=0), preferred_element_type=F32), first)

    def exchange(layer):
        kv_bf[layer] = acc[layer, 2].astype(BF)
        for k in range(2):
            launch(
                kv_bf.at[layer], ex_pair.at[layer, sec], pair_send.at[layer, k],
                pair_recv.at[layer, sec], (k, row, partner),
            )
        launch(acc.at[layer, 2], ex_kv.at[layer], ex_send.at[layer, 1], ex_recv.at[layer, 1], sibling)
        launch(stat.at[layer], ex_stat.at[layer], ex_send.at[layer, 2], ex_recv.at[layer, 2], sibling)
        launch(acc.at[layer, other], ex_q.at[layer], ex_send.at[layer, 0], ex_recv.at[layer, 0], sibling)

    def prepare_mask():
        qpos = lax.broadcasted_iota(jnp.int32, (TREE, TREE), 0)
        kpos = lax.broadcasted_iota(jnp.int32, (TREE, TREE), 1)
        top, left = qpos < BLOCK, kpos < BLOCK
        live = jnp.where(
            top,
            jnp.where(left, live_ref[0, 0, 0], live_ref[0, 0, 1]),
            jnp.where(left, live_ref[0, 1, 0], live_ref[0, 1, 1]),
        )
        allowed = (kpos <= qpos) & (qpos <= last_ref[...]) & (live > 0)
        mask[...] = jnp.where(allowed, 1.0, 0.0).astype(F32)

    def attend(layer):
        for n, place in enumerate((ex_q, ex_kv, ex_stat)):
            landed(place.at[layer], ex_recv.at[layer, n])
        lines = stat[layer] + ex_stat[layer]
        total = jnp.concatenate(
            [jnp.sum(lines[half * STAT:(half + 1) * STAT], axis=0, keepdims=True) for half in range(2)], axis=1
        )
        inverse = lax.rsqrt(total * (1.0 / D) + EPSILON)
        inverse = jnp.transpose(jnp.broadcast_to(inverse, (DH, TREE)))
        query = ((acc[layer, sec] + ex_q[layer]) * inverse).astype(BF)
        mine = ((acc[layer, 2] + ex_kv[layer]) * inverse).astype(BF)
        for k in range(2):
            landed(ex_pair.at[layer, k], pair_recv.at[layer, k])
        theirs = ((ex_pair[layer, 0].astype(F32) + ex_pair[layer, 1].astype(F32)) * inverse).astype(BF)
        keys = jnp.where(odd, theirs, mine)
        values = jnp.where(odd, mine, theirs)
        scores = lax.dot_general(
            query, keys, (((1,), (1,)), ((), ())), preferred_element_type=F32
        ) * DH ** (-0.5)
        scores = jnp.where(mask[...] > 0.5, scores, F32(-1e30))
        weights = jnp.exp(scores - jnp.max(scores, axis=1, keepdims=True))
        probs = (weights / jnp.sum(weights, axis=1, keepdims=True)).astype(BF)
        mixed = jnp.dot(probs, values, preferred_element_type=F32).astype(BF)
        for h in range(2):
            mbuf[layer, h, cx, cy] = mixed[h * BLOCK:(h + 1) * BLOCK]

    def project(layer, h, d, first):
        if h == 0:
            x = xs[d]
            blocks = [mbuf[layer, 0, x, y] for y in range(SIDE)]
            right = [w_out[layer, x, y] for y in range(SIDE)]
        else:
            y = ys[d]
            blocks = [mbuf[layer, 1, x, y] for x in range(SIDE)]
            right = [w_out[layer, x, y] for x in range(SIDE)]
        left = jnp.concatenate(blocks, axis=1)
        part = jnp.dot(left, jnp.concatenate(right, axis=0), preferred_element_type=F32)
        for g in range(2):
            cols = slice(g * HALF, (g + 1) * HALF)
            if first:
                acc_o[layer, g, h * BLOCK:(h + 1) * BLOCK] = part[:, cols]
            else:
                acc_o[layer, g, h * BLOCK:(h + 1) * BLOCK] += part[:, cols]

    X = (xbuf, x_send, x_recv)
    M = (mbuf, m_send, m_recv)

    start_ring(0, 0)
    landed(gains.at[other], gain_recv)
    tok_copy.wait()
    prepare_x(0, half_of(tok_ref[...]).astype(F32))
    phase_one(*X, 0)
    prepare_mask()
    phase_two(*X, 0)
    relay(0, 0, 1)
    relay(0, 0, 2)
    start_ring(0, 1)
    for d in range(1, SIDE):
        for h in range(2):
            group_landed(xbuf, x_recv, 0, h, d)
    for i in range(2):
        add_chunk(0, 0, 0, i, i == 0)
    for d in range(1, 3):
        for way in range(2):
            for i in range(2):
                add_chunk(0, d, way, i, False)
    relay(0, 0, 3)
    relay(0, 1, 1)
    for way in range(2):
        for i in range(2):
            add_chunk(0, 3, way, i, False)
    relay(0, 0, 4)
    for i in range(2):
        add_chunk(0, 4, 0, i, False)
    exchange(0)
    start_ring(1, 0)
    relay(0, 1, 2)
    attend(0)
    phase_one(*M, 0)
    relay(0, 1, 3)
    phase_two(*M, 0)
    relay(1, 0, 1)
    relay(0, 1, 4)
    for h in range(2):
        project(0, h, 0, True)
    for d in range(1, SIDE):
        for h in range(2):
            group_landed(mbuf, m_recv, 0, h, d)
            project(0, h, d, False)
    launch(acc_o.at[0, other], ex_o, o_send, o_recv, sibling)
    start_ring(1, 1)
    landed(ex_o, o_recv)
    x1 = (half_of(tok_ref[...]).astype(F32) + (acc_o[0, sec] + ex_o[...])).astype(BF)
    x1buf[sec] = x1
    prepare_x(1, x1.astype(F32))
    phase_one(*X, 1)
    launch(x1buf.at[sec], x1buf.at[sec], x1_send, x1_recv, sibling)
    relay(1, 0, 2)
    phase_two(*X, 1)
    relay(1, 1, 1)
    relay(1, 0, 3)
    landed(x1buf.at[other], x1_recv)

    @pl.when(sec == 0)
    def _():
        for h in range(2):
            out_ref[0, :, h * HALF:(h + 1) * HALF] = x1buf[h]

    relay(1, 1, 2)
    relay(1, 0, 4)
    for h in range(2):
        add_group(1, h, 0, h == 0)
    for d in range(1, SIDE):
        for h in range(2):
            group_landed(xbuf, x_recv, 1, h, d)
            add_group(1, h, d, False)
    exchange(1)
    relay(1, 1, 3)
    attend(1)
    phase_one(*M, 1)
    phase_two(*M, 1)
    relay(1, 1, 4)
    for h in range(2):
        project(1, h, 0, True)
    for d in range(1, SIDE):
        for h in range(2):
            group_landed(mbuf, m_recv, 1, h, d)
            project(1, h, d, False)
    last_copy = remote(acc_o.at[1], ex_last, last_send, last_recv, (1, row, col))

    @pl.when(sec == 0)
    def _():
        last_copy.start()

    @pl.when(sec == 1)
    def _():
        last_copy.wait_recv()
        for h in range(2):
            x = x1buf[h].astype(F32)
            out_ref[0, :, h * HALF:(h + 1) * HALF] = (x + (acc_o[1, h] + ex_last[h])).astype(BF)

    for copy in ends:
        copy.wait_send()

    @pl.when(sec == 0)
    def _():
        last_copy.wait_send()


def shards(tokens, norm_gain, w_query, w_keyval, w_out, subtree_last, block_live):
    vmem = pl.BlockSpec(memory_space=pltpu.VMEM)
    hbm = pl.BlockSpec(memory_space=pltpu.HBM)
    dma = pltpu.SemaphoreType.DMA
    return pl.pallas_call(
        kernel,
        out_shape=jax.ShapeDtypeStruct((1, TREE, 2 * HALF), BF),
        in_specs=[hbm, vmem, hbm, hbm, hbm, vmem, pl.BlockSpec(memory_space=pltpu.SMEM)],
        out_specs=vmem,
        scratch_shapes=[
            pltpu.VMEM((2, SIDE, SIDE, HALF, 3 * DH), BF),
            pltpu.VMEM((2, SIDE, SIDE, DH, 2 * HALF), BF),
            pltpu.VMEM((TREE, 2 * HALF), BF),
            pltpu.VMEM((2, 2, SIDE, SIDE, TREE + 2 * STAT, DH), BF),
            pltpu.VMEM((2, 2, SIDE, SIDE, BLOCK, DH), BF),
            pltpu.VMEM((2, 8, 2 * HALF), F32),
            pltpu.VMEM((2, 3, TREE, DH), F32),
            pltpu.VMEM((2, 2, TREE, HALF), F32),
            pltpu.VMEM((2, TREE, DH), F32),
            pltpu.VMEM((2, TREE, DH), F32),
            pltpu.VMEM((2, 2, TREE, DH), BF),
            pltpu.VMEM((2, TREE, DH), BF),
            pltpu.VMEM((2, 2 * STAT, DH), F32),
            pltpu.VMEM((2, 2 * STAT, DH), F32),
            pltpu.VMEM((TREE, HALF), F32),
            pltpu.VMEM((2, TREE, HALF), F32),
            pltpu.VMEM((2, TREE, HALF), BF),
            pltpu.VMEM((TREE, TREE), F32),
            dma,
            dma((2, 2, 4, PARTS)), dma((2, SIDE, SIDE, 2)), dma((2, 2, 4, PARTS)), dma((2, SIDE, SIDE, 2)),
            dma((6,)), dma((2, 6)), dma, dma,
            dma((2, 2, 5, SIDE)), dma((2, 2, SIDE, SIDE)), dma((2, 2, 5, SIDE)), dma((2, 2, SIDE, SIDE)),
            dma((2, 3)), dma((2, 3)), dma((2, 2)), dma((2, 2)),
            dma, dma, dma, dma, dma, dma,
        ],
        compiler_params=pltpu.CompilerParams(
            collective_id=0, has_side_effects=True, vmem_limit_bytes=60 << 20
        ),
    )(
        tokens, norm_gain, w_query[0], w_keyval[0], w_out[0],
        subtree_last.reshape(1, TREE), block_live,
    )


def solution(mesh):
    in_specs = (
        P("row", "col"),
        P("section", "col"),
        P("section", "row", "col"),
        P("section", "row", "col"),
        P("section", "row", "col"),
        P("row"),
        P("row", None, None),
    )
    out_specs = P("section", "row", "col")
    return jax.shard_map(shards, mesh=mesh, in_specs=in_specs, out_specs=out_specs, check_vma=False)
```

```python
import jax
import jax.numpy as jnp
from jax import lax
from jax.experimental import pallas as pl
from jax.experimental.pallas import tpu as pltpu
from jax.sharding import PartitionSpec as P

MESH = pl.DeviceIdType.MESH
D = 8192
DH = 128
BLOCK = 128
TREE = 256
ROWS = 8
COLS = 16
SIDE = 4
HALF = 256
STAT = 16
PARTS = 4
EPSILON = 1e-05
BF = jnp.bfloat16
F32 = jnp.float32


def kernel(
    tok_hbm, gain_ref, wq_ref, wkv_ref, wo_ref, last_ref, live_ref, out_ref,
    w_in, w_out, tok_ref, xbuf, mbuf, gains, acc, acc_o, ex_q, ex_kv, ex_pair, kv_bf, stat, ex_stat,
    ex_o, ex_last, x1buf, mask, tok_sem,
    wi_send, wi_recv, wo_send, wo_recv, own_send, own_sem, gain_send, gain_recv,
    x_send, x_recv, m_send, m_recv, ex_send, ex_recv, pair_send, pair_recv,
    o_send, o_recv, last_send, last_recv, x1_send, x1_recv,
):
    sec = lax.axis_index("section")
    row = lax.axis_index("row")
    col = lax.axis_index("col")
    other = 1 - sec
    cx, cy = col // SIDE, lax.rem(col, SIDE)
    odd = lax.rem(col, 2) == 1
    partner = jnp.where(odd, col - 1, col + 1)
    sibling = (other, row, col)
    up = (sec, lax.rem(row + 1, ROWS), col)
    down = (sec, lax.rem(row + ROWS - 1, ROWS), col)
    xs = [cx] + [lax.rem(cx + d, SIDE) for d in range(1, SIDE)]
    ys = [cy] + [lax.rem(cy + d, SIDE) for d in range(1, SIDE)]
    along_x = [(sec, row, x * SIDE + cy) for x in xs]
    along_y = [(sec, row, cx * SIDE + y) for y in ys]
    ends = []

    def remote(src, dst, send, recv, device):
        return pltpu.make_async_remote_copy(
            src_ref=src, dst_ref=dst, send_sem=send, recv_sem=recv, device_id=device, device_id_type=MESH
        )

    def launch(src, dst, send, recv, device):
        copy = remote(src, dst, send, recv, device)
        copy.start()
        ends.append(copy)
        return copy

    def landed(place, recv):
        remote(place, place, gain_send, recv, sibling).wait_recv()

    tok_copy = pltpu.make_async_copy(tok_hbm, tok_ref, tok_sem)
    tok_copy.start()
    barrier = pltpu.get_barrier_semaphore()
    greeted = [sibling, up, down, (other, row, partner)] + along_x[1:] + along_y[1:]
    for device in greeted:
        pl.semaphore_signal(barrier, 1, device_id=device, device_id_type=MESH)

    def slot_of(origin, i):
        return origin // 2, 2 * lax.rem(origin, 2) + i

    def half_of(x):
        return jnp.where(sec == 0, x[:, :HALF], x[:, HALF:])

    def prepare_stat(layer, x):
        square = x * x
        high = square.astype(BF)
        low = (square - high.astype(F32)).astype(BF)
        ones = jnp.ones((STAT, DH), BF)
        dims = (((1,), (1,)), ((), ()))
        line = lax.broadcasted_iota(jnp.int32, (STAT, DH), 0)
        for h in range(2):
            cols = slice(h * DH, (h + 1) * DH)
            total = lax.dot_general(ones, high[:, cols], dims, preferred_element_type=F32)
            total += lax.dot_general(ones, low[:, cols], dims, preferred_element_type=F32)
            top = total.astype(BF).astype(F32)
            rest = total - top
            rows = jnp.zeros((STAT, DH), F32)
            for n, part in enumerate((top[:, :DH], rest[:, :DH], top[:, DH:], rest[:, DH:])):
                rows = jnp.where(line == n, part, rows)
            xbuf[layer, h, cx, cy, TREE:] = rows.astype(BF)

    def prepare_mask():
        qpos = lax.broadcasted_iota(jnp.int32, (TREE, TREE), 0)
        kpos = lax.broadcasted_iota(jnp.int32, (TREE, TREE), 1)
        top, left = qpos < BLOCK, kpos < BLOCK
        live = jnp.where(
            top,
            jnp.where(left, live_ref[0, 0, 0], live_ref[0, 0, 1]),
            jnp.where(left, live_ref[0, 1, 0], live_ref[0, 1, 1]),
        )
        allowed = (kpos <= qpos) & (qpos <= last_ref[...]) & (live > 0)
        mask[...] = jnp.where(allowed, 1.0, 0.0).astype(F32)

    def before_barrier():
        prepare_mask()
        tok_copy.wait()
        prepare_stat(0, half_of(tok_ref[...]).astype(F32))

    def own_parts(half, kind):
        parts = []
        for i in range(2):
            sx, sy = slot_of(row, i)
            if kind == 0:
                base = pl.multiple_of(i * 512 + half * HALF, HALF)
                parts.append((wq_ref.at[pl.ds(base, HALF)], w_in.at[sec, sx, sy, :, pl.ds(0, 256)]))
                parts.append((wkv_ref.at[pl.ds(base, HALF)], w_in.at[sec, sx, sy, :, pl.ds(256, 128)]))
            else:
                base = pl.multiple_of(i * 256 + half * 128, 128)
                parts.append((wo_ref.at[pl.ds(base, 128)], w_out.at[sec, sx, sy]))
        return parts

    swaps, keeps = [], []
    n = 0
    for kind in range(2):
        for (src, dst), (mine, place) in zip(own_parts(other, kind), own_parts(sec, kind)):
            swaps.append((src, dst, own_send.at[n], own_sem.at[sec, n], sibling))
            keeps.append(pltpu.make_async_copy(mine, place, own_sem.at[sec, n]))
            n += 1
    for copy in keeps:
        copy.start()
    gains[sec] = jnp.broadcast_to(gain_ref[...].astype(F32), (8, 2 * HALF))
    before_barrier()
    pl.semaphore_wait(barrier, len(greeted))
    for swap in swaps[:4]:
        launch(*swap)
    launch(gains.at[sec], gains.at[sec], gain_send, gain_recv, sibling)
    for swap in swaps[4:]:
        launch(*swap)

    def wait_own(s, kind):
        for n in range(4) if kind == 0 else range(4, 6):
            sx, sy = slot_of(row, n // 2 if kind == 0 else n - 4)
            if kind == 0:
                place = w_in.at[s, sx, sy, :, pl.ds(0, 256) if n % 2 == 0 else pl.ds(256, 128)]
            else:
                place = w_out.at[s, sx, sy]
            pltpu.make_async_copy(place, place, own_sem.at[s, n]).wait()

    origins = {(0, 0): row, (0, 1): row}
    for d in range(1, 5):
        origins[d, 0] = lax.rem(row + ROWS - d, ROWS)
        origins[d, 1] = lax.rem(row + d, ROWS)

    def chunk(s, kind, d, way, i):
        buf, send, recv = (w_in, wi_send, wi_recv) if kind == 0 else (w_out, wo_send, wo_recv)
        sx, sy = slot_of(origins[d, way], i // 2)
        rows = (HALF if kind == 0 else DH) // 2
        place = buf.at[s, sx, sy, pl.ds(i % 2 * rows, rows)]
        return place, send.at[s, way, d, i], recv.at[s, sx, sy, i % 2]

    def forward(s, kind, d, way, i):
        place, send, recv = chunk(s, kind, d, way, i)
        launch(place, place, send, recv, up if way == 0 else down)

    def start_ring(s, kind):
        wait_own(s, kind)
        for i in range(PARTS):
            for way in range(2):
                forward(s, kind, 0, way, i)

    def relay(s, kind, d):
        for i in range(PARTS):
            for way in range(2):
                if d < 4 or i % 2 == way:
                    place, send, recv = chunk(s, kind, d, way, i)
                    landed(place, recv)
                    if d < 3 or (d == 3 and i % 2 == way):
                        forward(s, kind, d, way, i)

    X = (xbuf, x_send, x_recv)
    M = (mbuf, m_send, m_recv)

    def block_of(buf, recv, layer, h, along, across):
        x, y = (xs[across], ys[along]) if h == 0 else (xs[along], ys[across])
        return buf.at[layer, h, x, y], recv.at[layer, h, x, y]

    def phase_one(buf, send, recv, layer, halves=(0, 1)):
        for n, lines in ((SIDE, (along_y, along_x)), (0, (along_x, along_y))):
            for d in range(1, SIDE):
                for h in halves:
                    block, sem = block_of(buf, recv, layer, h, 0, 0)
                    launch(block, block, send.at[layer, h, n, d], sem, lines[h][d])

    def phase_two(buf, send, recv, layer):
        for j in (1, 3, 2):
            for h in range(2):
                block, sem = block_of(buf, recv, layer, h, j, 0)
                landed(block, sem)
                for d in range(1, SIDE):
                    launch(block, block, send.at[layer, h, j, d], sem, (along_x, along_y)[h][d])

    def group_landed(buf, recv, layer, h, d):
        for j in range(SIDE):
            landed(*block_of(buf, recv, layer, h, j, d))

    def prepare_x(layer, x):
        scaled = (x * half_of(gains[layer])[0:1]).astype(BF)
        for h in range(2):
            xbuf[layer, h, cx, cy, :TREE] = scaled[:, h * DH:(h + 1) * DH]

    def add_stat(layer, blocks, first):
        lines = blocks[0][TREE:].astype(F32)
        for block in blocks[1:]:
            lines += block[TREE:].astype(F32)
        if first:
            stat[layer] = lines
        else:
            stat[layer] += lines

    def add_part(layer, part, first):
        for g in range(3):
            if first:
                acc[layer, g] = part[:, g * DH:(g + 1) * DH]
            else:
                acc[layer, g] += part[:, g * DH:(g + 1) * DH]

    def add_pair(layer, sx, sy, first=False):
        blocks = [xbuf[layer, h, sx, sy + i] for i in range(2) for h in range(2)]
        left = jnp.concatenate([block[:TREE] for block in blocks], axis=1)
        right = jnp.concatenate([w_in[layer, sx, sy + i] for i in range(2)], axis=0)
        add_stat(layer, blocks, first)
        add_part(layer, jnp.dot(left, right, preferred_element_type=F32), first)

    def exchange(layer):
        kv_bf[layer] = acc[layer, 2].astype(BF)
        for k in range(2):
            launch(
                kv_bf.at[layer], ex_pair.at[layer, sec], pair_send.at[layer, k],
                pair_recv.at[layer, sec], (k, row, partner),
            )
        launch(acc.at[layer, 2], ex_kv.at[layer], ex_send.at[layer, 1], ex_recv.at[layer, 1], sibling)
        launch(stat.at[layer], ex_stat.at[layer], ex_send.at[layer, 2], ex_recv.at[layer, 2], sibling)
        launch(acc.at[layer, other], ex_q.at[layer], ex_send.at[layer, 0], ex_recv.at[layer, 0], sibling)

    def attend(layer):
        for n, place in enumerate((ex_q, ex_kv, ex_stat)):
            landed(place.at[layer], ex_recv.at[layer, n])
        lines = stat[layer] + ex_stat[layer]
        total = jnp.concatenate(
            [lines[2 * half:2 * half + 1] + lines[2 * half + 1:2 * half + 2] for half in range(2)], axis=1
        )
        inverse = lax.rsqrt(total * (1.0 / D) + EPSILON)
        inverse = jnp.transpose(jnp.broadcast_to(inverse, (DH, TREE)))
        query = ((acc[layer, sec] + ex_q[layer]) * inverse).astype(BF)
        mine = ((acc[layer, 2] + ex_kv[layer]) * inverse).astype(BF)
        for k in range(2):
            landed(ex_pair.at[layer, k], pair_recv.at[layer, k])
        theirs = ((ex_pair[layer, 0].astype(F32) + ex_pair[layer, 1].astype(F32)) * inverse).astype(BF)
        keys = jnp.where(odd, theirs, mine)
        values = jnp.where(odd, mine, theirs)
        for h in range(2):
            seen = BLOCK * (h + 1)
            rows = slice(h * BLOCK, seen)
            scores = lax.dot_general(
                query[rows], keys[:seen], (((1,), (1,)), ((), ())), preferred_element_type=F32
            ) * DH ** (-0.5)
            scores = jnp.where(mask[rows, :seen] > 0.5, scores, F32(-1e30))
            weights = jnp.exp(scores - jnp.max(scores, axis=1, keepdims=True))
            probs = (weights / jnp.sum(weights, axis=1, keepdims=True)).astype(BF)
            mbuf[layer, h, cx, cy] = jnp.dot(probs, values[:seen], preferred_element_type=F32).astype(BF)
            phase_one(*M, layer, (h,))

    def project_pair(layer, sx, sy, first=False):
        rows = []
        for h in range(2):
            rows.append(jnp.concatenate([mbuf[layer, h, sx, sy + i] for i in range(2)], axis=1))
        right = jnp.concatenate([w_out[layer, sx, sy + i] for i in range(2)], axis=0)
        part = jnp.dot(jnp.concatenate(rows, axis=0), right, preferred_element_type=F32)
        for g in range(2):
            cols = slice(g * HALF, (g + 1) * HALF)
            if first:
                acc_o[layer, g] = part[:, cols]
            else:
                acc_o[layer, g] += part[:, cols]

    def all_landed(buf, recv, layer):
        for d in range(1, SIDE):
            for h in range(2):
                group_landed(buf, recv, layer, h, d)

    def near(work, layer, most=3, least=0):
        for d in range(least, most + 1):
            for way in range(2) if 0 < d < 4 else range(1):
                work(layer, *slot_of(origins[d, way], 0), d == 0)

    def flow(work, buf, recv, layer):
        for n, j in enumerate((0, 1, 3, 2)):
            for pair in range(0, SIDE, 2):
                for y in (pair, pair + 1):
                    if j:
                        landed(buf.at[layer, 0, xs[j], y], recv.at[layer, 0, xs[j], y])

                    @pl.when(cy != y)
                    def _():
                        landed(buf.at[layer, 1, xs[j], y], recv.at[layer, 1, xs[j], y])

                work(layer, xs[j], pair, n == 0 and pair == 0)

    start_ring(0, 0)
    landed(gains.at[other], gain_recv)
    prepare_x(0, half_of(tok_ref[...]).astype(F32))
    phase_one(*X, 0)
    phase_two(*X, 0)
    relay(0, 0, 1)
    relay(0, 0, 2)
    start_ring(0, 1)
    all_landed(xbuf, x_recv, 0)
    near(add_pair, 0, 2)
    relay(0, 0, 3)
    near(add_pair, 0, 3, 3)
    relay(0, 1, 1)
    start_ring(1, 0)
    relay(0, 0, 4)
    near(add_pair, 0, 4, 4)
    exchange(0)
    relay(0, 1, 2)
    attend(0)
    relay(0, 1, 3)
    phase_two(*M, 0)
    relay(1, 0, 1)
    relay(0, 1, 4)
    flow(project_pair, mbuf, m_recv, 0)
    launch(acc_o.at[0, other], ex_o, o_send, o_recv, sibling)
    landed(ex_o, o_recv)
    x1 = (half_of(tok_ref[...]).astype(F32) + (acc_o[0, sec] + ex_o[...])).astype(BF)
    x1buf[sec] = x1
    prepare_x(1, x1.astype(F32))
    prepare_stat(1, x1.astype(F32))
    phase_one(*X, 1)
    launch(x1buf.at[sec], x1buf.at[sec], x1_send, x1_recv, sibling)
    relay(1, 0, 2)
    phase_two(*X, 1)
    landed(x1buf.at[other], x1_recv)

    @pl.when(sec == 0)
    def _():
        for h in range(2):
            out_ref[0, :, h * HALF:(h + 1) * HALF] = x1buf[h]

    relay(1, 0, 3)
    start_ring(1, 1)
    relay(1, 0, 4)
    flow(add_pair, xbuf, x_recv, 1)
    exchange(1)
    relay(1, 1, 1)
    attend(1)
    relay(1, 1, 2)
    phase_two(*M, 1)
    relay(1, 1, 3)
    all_landed(mbuf, m_recv, 1)
    near(project_pair, 1)
    relay(1, 1, 4)
    near(project_pair, 1, 4, 4)
    last_copy = remote(acc_o.at[1], ex_last, last_send, last_recv, (1, row, col))

    @pl.when(sec == 0)
    def _():
        last_copy.start()

    @pl.when(sec == 1)
    def _():
        last_copy.wait_recv()
        for h in range(2):
            x = x1buf[h].astype(F32)
            out_ref[0, :, h * HALF:(h + 1) * HALF] = (x + (acc_o[1, h] + ex_last[h])).astype(BF)

    for copy in ends:
        copy.wait_send()

    @pl.when(sec == 0)
    def _():
        last_copy.wait_send()


def shards(tokens, norm_gain, w_query, w_keyval, w_out, subtree_last, block_live):
    vmem = pl.BlockSpec(memory_space=pltpu.VMEM)
    hbm = pl.BlockSpec(memory_space=pltpu.HBM)
    dma = pltpu.SemaphoreType.DMA
    return pl.pallas_call(
        kernel,
        out_shape=pltpu.VMEM((1, TREE, 2 * HALF), BF),
        in_specs=[hbm, vmem, hbm, hbm, hbm, vmem, pl.BlockSpec(memory_space=pltpu.SMEM)],
        out_specs=vmem,
        scratch_shapes=[
            pltpu.VMEM((2, SIDE, SIDE, HALF, 3 * DH), BF),
            pltpu.VMEM((2, SIDE, SIDE, DH, 2 * HALF), BF),
            pltpu.VMEM((TREE, 2 * HALF), BF),
            pltpu.VMEM((2, 2, SIDE, SIDE, TREE + STAT, DH), BF),
            pltpu.VMEM((2, 2, SIDE, SIDE, BLOCK, DH), BF),
            pltpu.VMEM((2, 8, 2 * HALF), F32),
            pltpu.VMEM((2, 3, TREE, DH), F32),
            pltpu.VMEM((2, 2, TREE, HALF), F32),
            pltpu.VMEM((2, TREE, DH), F32),
            pltpu.VMEM((2, TREE, DH), F32),
            pltpu.VMEM((2, 2, TREE, DH), BF),
            pltpu.VMEM((2, TREE, DH), BF),
            pltpu.VMEM((2, STAT, DH), F32),
            pltpu.VMEM((2, STAT, DH), F32),
            pltpu.VMEM((TREE, HALF), F32),
            pltpu.VMEM((2, TREE, HALF), F32),
            pltpu.VMEM((2, TREE, HALF), BF),
            pltpu.VMEM((TREE, TREE), F32),
            dma,
            dma((2, 2, 4, PARTS)), dma((2, SIDE, SIDE, 2)), dma((2, 2, 4, PARTS)), dma((2, SIDE, SIDE, 2)),
            dma((6,)), dma((2, 6)), dma, dma,
            dma((2, 2, 5, SIDE)), dma((2, 2, SIDE, SIDE)), dma((2, 2, 5, SIDE)), dma((2, 2, SIDE, SIDE)),
            dma((2, 3)), dma((2, 3)), dma((2, 2)), dma((2, 2)),
            dma, dma, dma, dma, dma, dma,
        ],
        compiler_params=pltpu.CompilerParams(
            collective_id=0, has_side_effects=True, vmem_limit_bytes=60 << 20
        ),
    )(
        tokens, norm_gain, w_query[0], w_keyval[0], w_out[0],
        subtree_last.reshape(1, TREE), block_live,
    )


def solution(mesh):
    in_specs = (
        P("row", "col"),
        P("section", "col"),
        P("section", "row", "col"),
        P("section", "row", "col"),
        P("section", "row", "col"),
        P("row"),
        P("row", None, None),
    )
    out_specs = P("section", "row", "col")
    return jax.shard_map(shards, mesh=mesh, in_specs=in_specs, out_specs=out_specs, check_vma=False)
```

```python
import jax
import jax.numpy as jnp
from jax import lax
from jax.experimental import pallas as pl
from jax.experimental.pallas import tpu as pltpu
from jax.sharding import PartitionSpec as P

MESH = pl.DeviceIdType.MESH
D = 8192
DH = 128
BLOCK = 128
TREE = 256
ROWS = 8
COLS = 16
SIDE = 4
HALF = 256
STAT = 16
PARTS = 4
EPSILON = 1e-05
BF = jnp.bfloat16
F32 = jnp.float32


def kernel(
    tok_hbm, gain_ref, wq_ref, wkv_ref, wo_ref, last_ref, live_ref, out_ref,
    w_in, w_out, tok_ref, xbuf, mbuf, gains, acc, acc_o, ex_q, ex_kv, ex_pair, kv_bf, stat, ex_stat,
    ex_o, ex_last, x1buf, mask, tok_sem,
    wi_send, wi_recv, wo_send, wo_recv, own_send, own_sem, gain_send, gain_recv,
    x_send, x_recv, m_send, m_recv, ex_send, ex_recv, pair_send, pair_recv,
    o_send, o_recv, last_send, last_recv, x1_send, x1_recv,
):
    sec = lax.axis_index("section")
    row = lax.axis_index("row")
    col = lax.axis_index("col")
    other = 1 - sec
    cx, cy = col // SIDE, lax.rem(col, SIDE)
    odd = lax.rem(col, 2) == 1
    partner = jnp.where(odd, col - 1, col + 1)
    sibling = (other, row, col)
    up = (sec, lax.rem(row + jnp.where(sec == 0, 1, ROWS - 1), ROWS), col)
    down = (sec, lax.rem(row + jnp.where(sec == 0, ROWS - 1, 1), ROWS), col)
    xs = [cx] + [lax.rem(cx + d, SIDE) for d in range(1, SIDE)]
    ys = [cy] + [lax.rem(cy + d, SIDE) for d in range(1, SIDE)]
    along_x = [(sec, row, x * SIDE + cy) for x in xs]
    along_y = [(sec, row, cx * SIDE + y) for y in ys]
    ends = []

    def remote(src, dst, send, recv, device):
        return pltpu.make_async_remote_copy(
            src_ref=src, dst_ref=dst, send_sem=send, recv_sem=recv, device_id=device, device_id_type=MESH
        )

    def launch(src, dst, send, recv, device):
        copy = remote(src, dst, send, recv, device)
        copy.start()
        ends.append(copy)
        return copy

    def drain(keep=0):
        while len(ends) > keep:
            ends.pop(0).wait_send()

    def landed(place, recv):
        remote(place, place, gain_send, recv, sibling).wait_recv()

    tok_copy = pltpu.make_async_copy(tok_hbm, tok_ref, tok_sem)
    tok_copy.start()
    barrier = pltpu.get_barrier_semaphore()
    greeted = [sibling, up, down] + along_x[1:] + along_y[1:]
    for device in greeted:
        pl.semaphore_signal(barrier, 1, device_id=device, device_id_type=MESH)

    def slot_of(origin, i):
        return origin // 2, 2 * lax.rem(origin, 2) + i

    def half_of(x):
        return jnp.where(sec == 0, x[:, :HALF], x[:, HALF:])

    def prepare_stat(layer, x):
        square = x * x
        high = square.astype(BF)
        low = (square - high.astype(F32)).astype(BF)
        ones = jnp.ones((STAT, DH), BF)
        dims = (((1,), (1,)), ((), ()))
        line = lax.broadcasted_iota(jnp.int32, (STAT, DH), 0)
        for h in range(2):
            cols = slice(h * DH, (h + 1) * DH)
            total = lax.dot_general(ones, high[:, cols], dims, preferred_element_type=F32)
            total += lax.dot_general(ones, low[:, cols], dims, preferred_element_type=F32)
            top = total.astype(BF).astype(F32)
            rest = total - top
            rows = jnp.zeros((STAT, DH), F32)
            for n, part in enumerate((top[:, :DH], rest[:, :DH], top[:, DH:], rest[:, DH:])):
                rows = jnp.where(line == n, part, rows)
            xbuf[layer, h, cx, cy, TREE:] = rows.astype(BF)

    def prepare_mask():
        qpos = lax.broadcasted_iota(jnp.int32, (TREE, TREE), 0)
        kpos = lax.broadcasted_iota(jnp.int32, (TREE, TREE), 1)
        top, left = qpos < BLOCK, kpos < BLOCK
        live = jnp.where(
            top,
            jnp.where(left, live_ref[0, 0, 0], live_ref[0, 0, 1]),
            jnp.where(left, live_ref[0, 1, 0], live_ref[0, 1, 1]),
        )
        allowed = (kpos <= qpos) & (qpos <= last_ref[...]) & (live > 0)
        mask[...] = jnp.where(allowed, 1.0, 0.0).astype(F32)

    def before_barrier():
        prepare_mask()
        tok_copy.wait()
        prepare_stat(0, half_of(tok_ref[...]).astype(F32))

    def own_parts(half, kind):
        parts = []
        for i in range(2):
            sx, sy = slot_of(row, i)
            if kind == 0:
                base = pl.multiple_of(i * 512 + half * HALF, HALF)
                parts.append((wq_ref.at[pl.ds(base, HALF)], w_in.at[sec, sx, sy, :, pl.ds(0, 256)]))
                parts.append((wkv_ref.at[pl.ds(base, HALF)], w_in.at[sec, sx, sy, :, pl.ds(256, 128)]))
            else:
                base = pl.multiple_of(i * 256 + half * 128, 128)
                parts.append((wo_ref.at[pl.ds(base, 128)], w_out.at[sec, sx, sy]))
        return parts

    swaps, keeps = [], []
    n = 0
    for kind in range(2):
        for (src, dst), (mine, place) in zip(own_parts(other, kind), own_parts(sec, kind)):
            swaps.append((src, dst, own_send.at[n], own_sem.at[sec, n], sibling))
            keeps.append(pltpu.make_async_copy(mine, place, own_sem.at[sec, n]))
            n += 1
    for copy in keeps:
        copy.start()
    gains[sec] = jnp.broadcast_to(gain_ref[...].astype(F32), (8, 2 * HALF))
    before_barrier()
    pl.semaphore_wait(barrier, len(greeted))
    for swap in swaps[:4]:
        launch(*swap)
    launch(gains.at[sec], gains.at[sec], gain_send, gain_recv, sibling)
    for swap in swaps[4:]:
        launch(*swap)

    def wait_own(s, kind):
        for n in range(4) if kind == 0 else range(4, 6):
            sx, sy = slot_of(row, n // 2 if kind == 0 else n - 4)
            if kind == 0:
                place = w_in.at[s, sx, sy, :, pl.ds(0, 256) if n % 2 == 0 else pl.ds(256, 128)]
            else:
                place = w_out.at[s, sx, sy]
            pltpu.make_async_copy(place, place, own_sem.at[s, n]).wait()

    origins = {(0, 0): row, (0, 1): row}
    for d in range(1, 5):
        origins[d, 0] = lax.rem(row + jnp.where(sec == 0, ROWS - d, d), ROWS)
        origins[d, 1] = lax.rem(row + jnp.where(sec == 0, d, ROWS - d), ROWS)

    def chunk(s, kind, d, way, i):
        buf, send, recv = (w_in, wi_send, wi_recv) if kind == 0 else (w_out, wo_send, wo_recv)
        sx, sy = slot_of(origins[d, way], i // 2)
        rows = (HALF if kind == 0 else DH) // 2
        place = buf.at[s, sx, sy, pl.ds(i % 2 * rows, rows)]
        return place, send.at[s, way, d, i], recv.at[s, sx, sy, i % 2]

    def forward(s, kind, d, way, i):
        place, send, recv = chunk(s, kind, d, way, i)
        launch(place, place, send, recv, up if way == 0 else down)

    def start_ring(s, kind):
        wait_own(s, kind)
        for i in range(PARTS):
            for way in range(2):
                forward(s, kind, 0, way, i)

    def relay(s, kind, d, parts=range(PARTS)):
        for i in parts:
            for way in range(2):
                if d < 4 or i % 2 == way:
                    place, send, recv = chunk(s, kind, d, way, i)
                    landed(place, recv)
                    if d < 3 or (d == 3 and i % 2 == way):
                        forward(s, kind, d, way, i)

    X = (xbuf, x_send, x_recv)
    M = (mbuf, m_send, m_recv)

    def block_of(buf, recv, layer, h, along, across):
        x, y = (xs[across], ys[along]) if h == 0 else (xs[along], ys[across])
        return buf.at[layer, h, x, y], recv.at[layer, h, x, y]

    def phase_one(buf, send, recv, layer, halves=(0, 1)):
        for n, lines in ((SIDE, (along_y, along_x)), (0, (along_x, along_y))):
            for d in range(1, SIDE):
                for h in halves:
                    block, sem = block_of(buf, recv, layer, h, 0, 0)
                    launch(block, block, send.at[layer, h, n, d], sem, lines[h][d])

    def phase_two(buf, send, recv, layer, steps=(1, 3, 2)):
        for j in steps:
            for h in range(2):
                block, sem = block_of(buf, recv, layer, h, j, 0)
                landed(block, sem)
                for d in range(1, SIDE):
                    launch(block, block, send.at[layer, h, j, d], sem, (along_x, along_y)[h][d])

    def group_landed(buf, recv, layer, h, d):
        for j in range(SIDE):
            landed(*block_of(buf, recv, layer, h, j, d))

    def prepare_x(layer, x):
        scaled = (x * half_of(gains[layer])[0:1]).astype(BF)
        for h in range(2):
            xbuf[layer, h, cx, cy, :TREE] = scaled[:, h * DH:(h + 1) * DH]

    def add_stat(layer, blocks, first):
        lines = blocks[0][TREE:].astype(F32)
        for block in blocks[1:]:
            lines += block[TREE:].astype(F32)
        if first:
            stat[layer] = lines
        else:
            stat[layer] += lines

    def add_part(layer, part, first):
        for g in range(3):
            if first:
                acc[layer, g] = part[:, g * DH:(g + 1) * DH]
            else:
                acc[layer, g] += part[:, g * DH:(g + 1) * DH]

    def add_pair(layer, sx, sy, first=False):
        blocks = [xbuf[layer, h, sx, sy + i] for i in range(2) for h in range(2)]
        left = jnp.concatenate([block[:TREE] for block in blocks], axis=1)
        right = jnp.concatenate([w_in[layer, sx, sy + i] for i in range(2)], axis=0)
        add_stat(layer, blocks, first)
        add_part(layer, jnp.dot(left, right, preferred_element_type=F32), first)

    def exchange(layer):
        kv_bf[layer] = acc[layer, 2].astype(BF)
        launch(
            kv_bf.at[layer], ex_pair.at[layer, sec], pair_send.at[layer, 0], pair_recv.at[layer, 0], (sec, row, partner)
        )
        launch(acc.at[layer, 2], ex_kv.at[layer], ex_send.at[layer, 1], ex_recv.at[layer, 1], sibling)
        launch(stat.at[layer], ex_stat.at[layer], ex_send.at[layer, 2], ex_recv.at[layer, 2], sibling)
        launch(acc.at[layer, other], ex_q.at[layer], ex_send.at[layer, 0], ex_recv.at[layer, 0], sibling)

    def attend(layer):
        for n, place in enumerate((ex_q, ex_kv, ex_stat)):
            landed(place.at[layer], ex_recv.at[layer, n])
        lines = stat[layer] + ex_stat[layer]
        total = jnp.concatenate(
            [lines[2 * half:2 * half + 1] + lines[2 * half + 1:2 * half + 2] for half in range(2)], axis=1
        )
        inverse = lax.rsqrt(total * (1.0 / D) + EPSILON)
        inverse = jnp.transpose(jnp.broadcast_to(inverse, (DH, TREE)))
        query = ((acc[layer, sec] + ex_q[layer]) * inverse).astype(BF)
        mine = ((acc[layer, 2] + ex_kv[layer]) * inverse).astype(BF)
        place = ex_pair.at[layer, sec]
        landed(place, pair_recv.at[layer, 0])
        launch(place, place, pair_send.at[layer, 1], pair_recv.at[layer, 1], sibling)
        landed(ex_pair.at[layer, other], pair_recv.at[layer, 1])
        theirs = ((ex_pair[layer, 0].astype(F32) + ex_pair[layer, 1].astype(F32)) * inverse).astype(BF)
        keys = jnp.where(odd, theirs, mine)
        values = jnp.where(odd, mine, theirs)
        for h in range(2):
            seen = BLOCK * (h + 1)
            rows = slice(h * BLOCK, seen)
            scores = lax.dot_general(
                query[rows], keys[:seen], (((1,), (1,)), ((), ())), preferred_element_type=F32
            ) * DH ** (-0.5)
            scores = jnp.where(mask[rows, :seen] > 0.5, scores, F32(-1e30))
            weights = jnp.exp(scores - jnp.max(scores, axis=1, keepdims=True))
            probs = (weights / jnp.sum(weights, axis=1, keepdims=True)).astype(BF)
            mbuf[layer, h, cx, cy] = jnp.dot(probs, values[:seen], preferred_element_type=F32).astype(BF)
            phase_one(*M, layer, (h,))

    def project_pair(layer, sx, sy, first=False):
        rows = []
        for h in range(2):
            rows.append(jnp.concatenate([mbuf[layer, h, sx, sy + i] for i in range(2)], axis=1))
        right = jnp.concatenate([w_out[layer, sx, sy + i] for i in range(2)], axis=0)
        part = jnp.dot(jnp.concatenate(rows, axis=0), right, preferred_element_type=F32)
        for g in range(2):
            cols = slice(g * HALF, (g + 1) * HALF)
            if first:
                acc_o[layer, g] = part[:, cols]
            else:
                acc_o[layer, g] += part[:, cols]

    def all_landed(buf, recv, layer):
        for d in range(1, SIDE):
            for h in range(2):
                group_landed(buf, recv, layer, h, d)

    def near(work, layer, most=3, least=0):
        for d in range(least, most + 1):
            for way in range(2) if 0 < d < 4 else range(1):
                work(layer, *slot_of(origins[d, way], 0), d == 0)

    def flow(work, buf, recv, layer, steps=(0, 1, 3, 2)):
        for j in steps:
            for pair in range(0, SIDE, 2):
                for y in (pair, pair + 1):
                    if j:
                        landed(buf.at[layer, 0, xs[j], y], recv.at[layer, 0, xs[j], y])

                    @pl.when(cy != y)
                    def _():
                        landed(buf.at[layer, 1, xs[j], y], recv.at[layer, 1, xs[j], y])

                work(layer, xs[j], pair, j == 0 and pair == 0)

    start_ring(0, 0)
    landed(gains.at[other], gain_recv)
    prepare_x(0, half_of(tok_ref[...]).astype(F32))
    phase_one(*X, 0)
    phase_two(*X, 0)
    relay(0, 0, 1)
    relay(0, 0, 2)
    start_ring(0, 1)
    all_landed(xbuf, x_recv, 0)
    near(add_pair, 0, 2)
    relay(0, 0, 3)
    near(add_pair, 0, 3, 3)
    relay(0, 1, 1)
    start_ring(1, 0)
    relay(0, 0, 4)
    near(add_pair, 0, 4, 4)
    exchange(0)
    relay(0, 1, 2)
    attend(0)
    relay(0, 1, 3)
    relay(1, 0, 1)
    phase_two(*M, 0)
    relay(0, 1, 4)
    flow(project_pair, mbuf, m_recv, 0)
    launch(acc_o.at[0, other], ex_o, o_send, o_recv, sibling)
    landed(ex_o, o_recv)
    x1 = (half_of(tok_ref[...]).astype(F32) + (acc_o[0, sec] + ex_o[...])).astype(BF)
    x1buf[sec] = x1
    prepare_x(1, x1.astype(F32))
    prepare_stat(1, x1.astype(F32))
    phase_one(*X, 1)
    launch(x1buf.at[sec], x1buf.at[sec], x1_send, x1_recv, sibling)
    relay(1, 0, 2)
    phase_two(*X, 1)
    landed(x1buf.at[other], x1_recv)

    @pl.when(sec == 0)
    def _():
        for h in range(2):
            out_ref[0, :, h * HALF:(h + 1) * HALF] = x1buf[h]

    relay(1, 0, 3)
    start_ring(1, 1)
    relay(1, 0, 4)
    flow(add_pair, xbuf, x_recv, 1)
    exchange(1)
    relay(1, 1, 1)
    attend(1)
    relay(1, 1, 2)
    phase_two(*M, 1)
    relay(1, 1, 3)
    relay(1, 1, 4)
    flow(project_pair, mbuf, m_recv, 1)
    last_copies = [
        remote(acc_o.at[1, h], ex_last.at[h], last_send.at[h], last_recv.at[h], (1, row, col)) for h in range(2)
    ]

    @pl.when(sec == 0)
    def _():
        for copy in last_copies:
            copy.start()

    drain()

    @pl.when(sec == 1)
    def _():
        for h in range(2):
            last_copies[h].wait_recv()
            x = x1buf[h].astype(F32)
            out_ref[0, :, h * HALF:(h + 1) * HALF] = (x + (acc_o[1, h] + ex_last[h])).astype(BF)

    @pl.when(sec == 0)
    def _():
        for copy in last_copies:
            copy.wait_send()


def shards(tokens, norm_gain, w_query, w_keyval, w_out, subtree_last, block_live):
    vmem = pl.BlockSpec(memory_space=pltpu.VMEM)
    hbm = pl.BlockSpec(memory_space=pltpu.HBM)
    dma = pltpu.SemaphoreType.DMA
    return pl.pallas_call(
        kernel,
        out_shape=pltpu.VMEM((1, TREE, 2 * HALF), BF),
        in_specs=[hbm, vmem, hbm, hbm, hbm, vmem, pl.BlockSpec(memory_space=pltpu.SMEM)],
        out_specs=vmem,
        scratch_shapes=[
            pltpu.VMEM((2, SIDE, SIDE, HALF, 3 * DH), BF),
            pltpu.VMEM((2, SIDE, SIDE, DH, 2 * HALF), BF),
            pltpu.VMEM((TREE, 2 * HALF), BF),
            pltpu.VMEM((2, 2, SIDE, SIDE, TREE + STAT, DH), BF),
            pltpu.VMEM((2, 2, SIDE, SIDE, BLOCK, DH), BF),
            pltpu.VMEM((2, 8, 2 * HALF), F32),
            pltpu.VMEM((2, 3, TREE, DH), F32),
            pltpu.VMEM((2, 2, TREE, HALF), F32),
            pltpu.VMEM((2, TREE, DH), F32),
            pltpu.VMEM((2, TREE, DH), F32),
            pltpu.VMEM((2, 2, TREE, DH), BF),
            pltpu.VMEM((2, TREE, DH), BF),
            pltpu.VMEM((2, STAT, DH), F32),
            pltpu.VMEM((2, STAT, DH), F32),
            pltpu.VMEM((TREE, HALF), F32),
            pltpu.VMEM((2, TREE, HALF), F32),
            pltpu.VMEM((2, TREE, HALF), BF),
            pltpu.VMEM((TREE, TREE), F32),
            dma,
            dma((2, 2, 4, PARTS)), dma((2, SIDE, SIDE, 2)), dma((2, 2, 4, PARTS)), dma((2, SIDE, SIDE, 2)),
            dma((6,)), dma((2, 6)), dma, dma,
            dma((2, 2, 5, SIDE)), dma((2, 2, SIDE, SIDE)), dma((2, 2, 5, SIDE)), dma((2, 2, SIDE, SIDE)),
            dma((2, 3)), dma((2, 3)), dma((2, 2)), dma((2, 2)),
            dma, dma, dma((2,)), dma((2,)), dma, dma,
        ],
        compiler_params=pltpu.CompilerParams(
            collective_id=0, has_side_effects=True, vmem_limit_bytes=60 << 20
        ),
    )(
        tokens, norm_gain, w_query[0], w_keyval[0], w_out[0],
        subtree_last.reshape(1, TREE), block_live,
    )


def solution(mesh):
    in_specs = (
        P("row", "col"),
        P("section", "col"),
        P("section", "row", "col"),
        P("section", "row", "col"),
        P("section", "row", "col"),
        P("row"),
        P("row", None, None),
    )
    out_specs = P("section", "row", "col")
    return jax.shard_map(shards, mesh=mesh, in_specs=in_specs, out_specs=out_specs, check_vma=False)
```

```python
import jax
import jax.numpy as jnp
from jax import lax
from jax.experimental import pallas as pl
from jax.experimental.pallas import tpu as pltpu
from jax.sharding import PartitionSpec as P

MESH = pl.DeviceIdType.MESH
D = 8192
DH = 128
BLOCK = 128
TREE = 256
ROWS = 8
COLS = 16
SIDE = 4
HALF = 256
STAT = 16
PARTS = 4
EPSILON = 1e-05
BF = jnp.bfloat16
F32 = jnp.float32


def kernel(
    tok_hbm, gain_ref, wq_ref, wkv_ref, wo_ref, last_ref, live_ref, out_ref,
    w_in, w_out, tok_ref, xbuf, mbuf, gains, acc, acc_o, ex_q, ex_kv, ex_pair, kv_bf, stat, ex_stat,
    ex_o, ex_last, x1buf, mask, tok_sem,
    wi_send, wi_recv, wo_send, wo_recv, own_send, own_sem, gain_send, gain_recv,
    x_send, x_recv, m_send, m_recv, ex_send, ex_recv, pair_send, pair_recv,
    o_send, o_recv, last_send, last_recv, x1_send, x1_recv,
):
    sec = lax.axis_index("section")
    row = lax.axis_index("row")
    col = lax.axis_index("col")
    other = 1 - sec
    cx, cy = col // SIDE, lax.rem(col, SIDE)
    odd = lax.rem(col, 2) == 1
    partner = jnp.where(odd, col - 1, col + 1)
    sibling = (other, row, col)
    up = (sec, lax.rem(row + jnp.where(sec == 0, 1, ROWS - 1), ROWS), col)
    down = (sec, lax.rem(row + jnp.where(sec == 0, ROWS - 1, 1), ROWS), col)
    xs = [cx] + [lax.rem(cx + d, SIDE) for d in range(1, SIDE)]
    ys = [cy] + [lax.rem(cy + d, SIDE) for d in range(1, SIDE)]
    along_x = [(sec, row, x * SIDE + cy) for x in xs]
    along_y = [(sec, row, cx * SIDE + y) for y in ys]
    ends = []

    def remote(src, dst, send, recv, device):
        return pltpu.make_async_remote_copy(
            src_ref=src, dst_ref=dst, send_sem=send, recv_sem=recv, device_id=device, device_id_type=MESH
        )

    def launch(src, dst, send, recv, device):
        copy = remote(src, dst, send, recv, device)
        copy.start()
        ends.append(copy)
        return copy

    def drain(keep=0):
        while len(ends) > keep:
            ends.pop(0).wait_send()

    def landed(place, recv):
        remote(place, place, gain_send, recv, sibling).wait_recv()

    tok_copy = pltpu.make_async_copy(tok_hbm, tok_ref, tok_sem)
    tok_copy.start()
    barrier = pltpu.get_barrier_semaphore()
    greeted = [sibling, up, down] + along_x[1:] + along_y[1:]
    for device in greeted:
        pl.semaphore_signal(barrier, 1, device_id=device, device_id_type=MESH)

    def slot_of(origin, i):
        return origin // 2, 2 * lax.rem(origin, 2) + i

    def half_of(x):
        return jnp.where(sec == 0, x[:, :HALF], x[:, HALF:])

    def prepare_stat(layer, x):
        square = x * x
        high = square.astype(BF)
        low = (square - high.astype(F32)).astype(BF)
        ones = jnp.ones((STAT, DH), BF)
        dims = (((1,), (1,)), ((), ()))
        line = lax.broadcasted_iota(jnp.int32, (STAT, DH), 0)
        for h in range(2):
            cols = slice(h * DH, (h + 1) * DH)
            total = lax.dot_general(ones, high[:, cols], dims, preferred_element_type=F32)
            total += lax.dot_general(ones, low[:, cols], dims, preferred_element_type=F32)
            top = total.astype(BF).astype(F32)
            rest = total - top
            rows = jnp.zeros((STAT, DH), F32)
            for n, part in enumerate((top[:, :DH], rest[:, :DH], top[:, DH:], rest[:, DH:])):
                rows = jnp.where(line == n, part, rows)
            xbuf[layer, h, cx, cy, TREE:] = rows.astype(BF)

    def prepare_mask():
        qpos = lax.broadcasted_iota(jnp.int32, (TREE, TREE), 0)
        kpos = lax.broadcasted_iota(jnp.int32, (TREE, TREE), 1)
        top, left = qpos < BLOCK, kpos < BLOCK
        live = jnp.where(
            top,
            jnp.where(left, live_ref[0, 0, 0], live_ref[0, 0, 1]),
            jnp.where(left, live_ref[0, 1, 0], live_ref[0, 1, 1]),
        )
        allowed = (kpos <= qpos) & (qpos <= last_ref[...]) & (live > 0)
        mask[...] = jnp.where(allowed, 1.0, 0.0).astype(F32)

    def before_barrier():
        prepare_mask()
        tok_copy.wait()
        prepare_stat(0, half_of(tok_ref[...]).astype(F32))

    def own_parts(half, kind):
        parts = []
        for i in range(2):
            sx, sy = slot_of(row, i)
            if kind == 0:
                base = pl.multiple_of(i * 512 + half * HALF, HALF)
                parts.append((wq_ref.at[pl.ds(base, HALF)], w_in.at[sec, sx, sy, :, pl.ds(0, 256)]))
                parts.append((wkv_ref.at[pl.ds(base, HALF)], w_in.at[sec, sx, sy, :, pl.ds(256, 128)]))
            else:
                base = pl.multiple_of(i * 256 + half * 128, 128)
                parts.append((wo_ref.at[pl.ds(base, 128)], w_out.at[sec, sx, sy]))
        return parts

    swaps, keeps = [], []
    n = 0
    for kind in range(2):
        for (src, dst), (mine, place) in zip(own_parts(other, kind), own_parts(sec, kind)):
            swaps.append((src, dst, own_send.at[n], own_sem.at[sec, n], sibling))
            keeps.append(pltpu.make_async_copy(mine, place, own_sem.at[sec, n]))
            n += 1
    for copy in keeps:
        copy.start()
    gains[sec] = jnp.broadcast_to(gain_ref[...].astype(F32), (8, 2 * HALF))
    before_barrier()
    pl.semaphore_wait(barrier, len(greeted))
    for swap in swaps[:4]:
        launch(*swap)
    launch(gains.at[sec], gains.at[sec], gain_send, gain_recv, sibling)
    for swap in swaps[4:]:
        launch(*swap)

    def wait_own(s, kind):
        for n in range(4) if kind == 0 else range(4, 6):
            sx, sy = slot_of(row, n // 2 if kind == 0 else n - 4)
            if kind == 0:
                place = w_in.at[s, sx, sy, :, pl.ds(0, 256) if n % 2 == 0 else pl.ds(256, 128)]
            else:
                place = w_out.at[s, sx, sy]
            pltpu.make_async_copy(place, place, own_sem.at[s, n]).wait()

    origins = {(0, 0): row, (0, 1): row}
    for d in range(1, 5):
        origins[d, 0] = lax.rem(row + jnp.where(sec == 0, ROWS - d, d), ROWS)
        origins[d, 1] = lax.rem(row + jnp.where(sec == 0, d, ROWS - d), ROWS)

    def chunk(s, kind, d, way, i):
        buf, send, recv = (w_in, wi_send, wi_recv) if kind == 0 else (w_out, wo_send, wo_recv)
        sx, sy = slot_of(origins[d, way], i // 2)
        rows = (HALF if kind == 0 else DH) // 2
        place = buf.at[s, sx, sy, pl.ds(i % 2 * rows, rows)]
        return place, send.at[s, way, d, i], recv.at[s, sx, sy, i % 2]

    def forward(s, kind, d, way, i):
        place, send, recv = chunk(s, kind, d, way, i)
        launch(place, place, send, recv, up if way == 0 else down)

    def start_ring(s, kind):
        wait_own(s, kind)
        for i in range(PARTS):
            for way in range(2):
                forward(s, kind, 0, way, i)

    def relay(s, kind, d, parts=range(PARTS)):
        for i in parts:
            for way in range(2):
                if d < 4 or i % 2 == way:
                    place, send, recv = chunk(s, kind, d, way, i)
                    landed(place, recv)
                    if d < 3 or (d == 3 and i % 2 == way):
                        forward(s, kind, d, way, i)

    X = (xbuf, x_send, x_recv)
    M = (mbuf, m_send, m_recv)

    def block_of(buf, recv, layer, h, along, across):
        x, y = (xs[across], ys[along]) if h == 0 else (xs[along], ys[across])
        return buf.at[layer, h, x, y], recv.at[layer, h, x, y]

    def phase_one(buf, send, recv, layer, halves=(0, 1)):
        for n, lines in ((SIDE, (along_y, along_x)), (0, (along_x, along_y))):
            for d in range(1, SIDE):
                for h in halves:
                    block, sem = block_of(buf, recv, layer, h, 0, 0)
                    launch(block, block, send.at[layer, h, n, d], sem, lines[h][d])

    def phase_two(buf, send, recv, layer, steps=(1, 3, 2)):
        for j in steps:
            for h in range(2):
                block, sem = block_of(buf, recv, layer, h, j, 0)
                landed(block, sem)
                for d in range(1, SIDE):
                    launch(block, block, send.at[layer, h, j, d], sem, (along_x, along_y)[h][d])

    def group_landed(buf, recv, layer, h, d):
        for j in range(SIDE):
            landed(*block_of(buf, recv, layer, h, j, d))

    def prepare_x(layer, x):
        scaled = (x * half_of(gains[layer])[0:1]).astype(BF)
        for h in range(2):
            xbuf[layer, h, cx, cy, :TREE] = scaled[:, h * DH:(h + 1) * DH]

    def add_stat(layer, blocks, first):
        lines = blocks[0][TREE:].astype(F32)
        for block in blocks[1:]:
            lines += block[TREE:].astype(F32)
        if first:
            stat[layer] = lines
        else:
            stat[layer] += lines

    def add_part(layer, part, first):
        for g in range(3):
            if first:
                acc[layer, g] = part[:, g * DH:(g + 1) * DH]
            else:
                acc[layer, g] += part[:, g * DH:(g + 1) * DH]

    def add_pair(layer, sx, sy, first=False):
        blocks = [xbuf[layer, h, sx, sy + i] for i in range(2) for h in range(2)]
        left = jnp.concatenate([block[:TREE] for block in blocks], axis=1)
        right = jnp.concatenate([w_in[layer, sx, sy + i] for i in range(2)], axis=0)
        add_stat(layer, blocks, first)
        add_part(layer, jnp.dot(left, right, preferred_element_type=F32), first)

    def exchange(layer):
        kv_bf[layer] = acc[layer, 2].astype(BF)
        launch(
            kv_bf.at[layer], ex_pair.at[layer, sec], pair_send.at[layer, 0], pair_recv.at[layer, 0], (sec, row, partner)
        )
        launch(acc.at[layer, 2], ex_kv.at[layer], ex_send.at[layer, 1], ex_recv.at[layer, 1], sibling)
        launch(stat.at[layer], ex_stat.at[layer], ex_send.at[layer, 2], ex_recv.at[layer, 2], sibling)
        launch(acc.at[layer, other], ex_q.at[layer], ex_send.at[layer, 0], ex_recv.at[layer, 0], sibling)

    def attend(layer):
        for n, place in enumerate((ex_q, ex_kv, ex_stat)):
            landed(place.at[layer], ex_recv.at[layer, n])
        lines = stat[layer] + ex_stat[layer]
        total = jnp.concatenate(
            [lines[2 * half:2 * half + 1] + lines[2 * half + 1:2 * half + 2] for half in range(2)], axis=1
        )
        inverse = lax.rsqrt(total * (1.0 / D) + EPSILON)
        inverse = jnp.transpose(jnp.broadcast_to(inverse, (DH, TREE)))
        query = ((acc[layer, sec] + ex_q[layer]) * inverse).astype(BF)
        mine = ((acc[layer, 2] + ex_kv[layer]) * inverse).astype(BF)
        place = ex_pair.at[layer, sec]
        landed(place, pair_recv.at[layer, 0])
        launch(place, place, pair_send.at[layer, 1], pair_recv.at[layer, 1], sibling)
        landed(ex_pair.at[layer, other], pair_recv.at[layer, 1])
        theirs = ((ex_pair[layer, 0].astype(F32) + ex_pair[layer, 1].astype(F32)) * inverse).astype(BF)
        keys = jnp.where(odd, theirs, mine)
        values = jnp.where(odd, mine, theirs)
        for h in range(2):
            seen = BLOCK * (h + 1)
            rows = slice(h * BLOCK, seen)
            scores = lax.dot_general(
                query[rows], keys[:seen], (((1,), (1,)), ((), ())), preferred_element_type=F32
            ) * DH ** (-0.5)
            scores = jnp.where(mask[rows, :seen] > 0.5, scores, F32(-1e30))
            weights = jnp.exp(scores - jnp.max(scores, axis=1, keepdims=True))
            probs = (weights / jnp.sum(weights, axis=1, keepdims=True)).astype(BF)
            mbuf[layer, h, cx, cy] = jnp.dot(probs, values[:seen], preferred_element_type=F32).astype(BF)
            phase_one(*M, layer, (h,))

    def project_pair(layer, sx, sy, first=False):
        rows = []
        for h in range(2):
            rows.append(jnp.concatenate([mbuf[layer, h, sx, sy + i] for i in range(2)], axis=1))
        right = jnp.concatenate([w_out[layer, sx, sy + i] for i in range(2)], axis=0)
        part = jnp.dot(jnp.concatenate(rows, axis=0), right, preferred_element_type=F32)
        for g in range(2):
            cols = slice(g * HALF, (g + 1) * HALF)
            if first:
                acc_o[layer, g] = part[:, cols]
            else:
                acc_o[layer, g] += part[:, cols]

    def all_landed(buf, recv, layer):
        for d in range(1, SIDE):
            for h in range(2):
                group_landed(buf, recv, layer, h, d)

    def near(work, layer, most=3, least=0):
        for d in range(least, most + 1):
            for way in range(2) if 0 < d < 4 else range(1):
                work(layer, *slot_of(origins[d, way], 0), d == 0)

    def flow(work, buf, recv, layer, steps=(0, 1, 3, 2)):
        for j in steps:
            for pair in range(0, SIDE, 2):
                for y in (pair, pair + 1):
                    if j:
                        landed(buf.at[layer, 0, xs[j], y], recv.at[layer, 0, xs[j], y])

                    @pl.when(cy != y)
                    def _():
                        landed(buf.at[layer, 1, xs[j], y], recv.at[layer, 1, xs[j], y])

                work(layer, xs[j], pair, j == 0 and pair == 0)

    start_ring(0, 0)
    landed(gains.at[other], gain_recv)
    prepare_x(0, half_of(tok_ref[...]).astype(F32))
    phase_one(*X, 0)
    relay(0, 0, 1)
    phase_two(*X, 0)
    relay(0, 0, 2)
    start_ring(0, 1)
    all_landed(xbuf, x_recv, 0)
    near(add_pair, 0, 2)
    relay(0, 0, 3)
    near(add_pair, 0, 3, 3)
    relay(0, 1, 1)
    start_ring(1, 0)
    relay(0, 0, 4)
    near(add_pair, 0, 4, 4)
    exchange(0)
    relay(0, 1, 2)
    attend(0)
    relay(0, 1, 3)
    relay(1, 0, 1)
    phase_two(*M, 0)
    relay(0, 1, 4)
    flow(project_pair, mbuf, m_recv, 0)
    launch(acc_o.at[0, other], ex_o, o_send, o_recv, sibling)
    landed(ex_o, o_recv)
    x1 = (half_of(tok_ref[...]).astype(F32) + (acc_o[0, sec] + ex_o[...])).astype(BF)
    x1buf[sec] = x1
    prepare_x(1, x1.astype(F32))
    prepare_stat(1, x1.astype(F32))
    phase_one(*X, 1)
    launch(x1buf.at[sec], x1buf.at[sec], x1_send, x1_recv, sibling)
    relay(1, 0, 2)
    phase_two(*X, 1)
    landed(x1buf.at[other], x1_recv)

    @pl.when(sec == 0)
    def _():
        for h in range(2):
            out_ref[0, :, h * HALF:(h + 1) * HALF] = x1buf[h]

    relay(1, 0, 3)
    start_ring(1, 1)
    relay(1, 0, 4)
    flow(add_pair, xbuf, x_recv, 1)
    exchange(1)
    relay(1, 1, 1)
    attend(1)
    relay(1, 1, 2)
    phase_two(*M, 1)
    relay(1, 1, 3)
    all_landed(mbuf, m_recv, 1)
    near(project_pair, 1)
    relay(1, 1, 4)
    near(project_pair, 1, 4, 4)
    last_copies = [
        remote(acc_o.at[1, h], ex_last.at[h], last_send.at[h], last_recv.at[h], (1, row, col)) for h in range(2)
    ]

    @pl.when(sec == 0)
    def _():
        for copy in last_copies:
            copy.start()

    drain()

    @pl.when(sec == 1)
    def _():
        for h in range(2):
            last_copies[h].wait_recv()
            x = x1buf[h].astype(F32)
            out_ref[0, :, h * HALF:(h + 1) * HALF] = (x + (acc_o[1, h] + ex_last[h])).astype(BF)

    @pl.when(sec == 0)
    def _():
        for copy in last_copies:
            copy.wait_send()


def shards(tokens, norm_gain, w_query, w_keyval, w_out, subtree_last, block_live):
    vmem = pl.BlockSpec(memory_space=pltpu.VMEM)
    hbm = pl.BlockSpec(memory_space=pltpu.HBM)
    dma = pltpu.SemaphoreType.DMA
    return pl.pallas_call(
        kernel,
        out_shape=pltpu.VMEM((1, TREE, 2 * HALF), BF),
        in_specs=[hbm, vmem, hbm, hbm, hbm, vmem, pl.BlockSpec(memory_space=pltpu.SMEM)],
        out_specs=vmem,
        scratch_shapes=[
            pltpu.VMEM((2, SIDE, SIDE, HALF, 3 * DH), BF),
            pltpu.VMEM((2, SIDE, SIDE, DH, 2 * HALF), BF),
            pltpu.VMEM((TREE, 2 * HALF), BF),
            pltpu.VMEM((2, 2, SIDE, SIDE, TREE + STAT, DH), BF),
            pltpu.VMEM((2, 2, SIDE, SIDE, BLOCK, DH), BF),
            pltpu.VMEM((2, 8, 2 * HALF), F32),
            pltpu.VMEM((2, 3, TREE, DH), F32),
            pltpu.VMEM((2, 2, TREE, HALF), F32),
            pltpu.VMEM((2, TREE, DH), F32),
            pltpu.VMEM((2, TREE, DH), F32),
            pltpu.VMEM((2, 2, TREE, DH), BF),
            pltpu.VMEM((2, TREE, DH), BF),
            pltpu.VMEM((2, STAT, DH), F32),
            pltpu.VMEM((2, STAT, DH), F32),
            pltpu.VMEM((TREE, HALF), F32),
            pltpu.VMEM((2, TREE, HALF), F32),
            pltpu.VMEM((2, TREE, HALF), BF),
            pltpu.VMEM((TREE, TREE), F32),
            dma,
            dma((2, 2, 4, PARTS)), dma((2, SIDE, SIDE, 2)), dma((2, 2, 4, PARTS)), dma((2, SIDE, SIDE, 2)),
            dma((6,)), dma((2, 6)), dma, dma,
            dma((2, 2, 5, SIDE)), dma((2, 2, SIDE, SIDE)), dma((2, 2, 5, SIDE)), dma((2, 2, SIDE, SIDE)),
            dma((2, 3)), dma((2, 3)), dma((2, 2)), dma((2, 2)),
            dma, dma, dma((2,)), dma((2,)), dma, dma,
        ],
        compiler_params=pltpu.CompilerParams(
            collective_id=0, has_side_effects=True, vmem_limit_bytes=60 << 20
        ),
    )(
        tokens, norm_gain, w_query[0], w_keyval[0], w_out[0],
        subtree_last.reshape(1, TREE), block_live,
    )


def solution(mesh):
    in_specs = (
        P("row", "col"),
        P("section", "col"),
        P("section", "row", "col"),
        P("section", "row", "col"),
        P("section", "row", "col"),
        P("row"),
        P("row", None, None),
    )
    out_specs = P("section", "row", "col")
    return jax.shard_map(shards, mesh=mesh, in_specs=in_specs, out_specs=out_specs, check_vma=False)
```

```python
import jax
import jax.numpy as jnp
from jax import lax
from jax.experimental import pallas as pl
from jax.experimental.pallas import tpu as pltpu
from jax.sharding import PartitionSpec as P

MESH = pl.DeviceIdType.MESH
D = 8192
DH = 128
BLOCK = 128
TREE = 256
ROWS = 8
COLS = 16
SIDE = 4
HALF = 256
STAT = 16
PARTS = 4
EPSILON = 1e-05
BF = jnp.bfloat16
F32 = jnp.float32


def kernel(
    tok_hbm, gain_ref, wq_ref, wkv_ref, wo_ref, last_ref, live_ref, out_ref,
    w_in, w_out, tok_ref, xbuf, mbuf, gains, acc, acc_o, ex_q, ex_kv, ex_pair, kv_bf, stat, ex_stat,
    ex_o, ex_last, x1buf, mask, tok_sem,
    wi_send, wi_recv, wo_send, wo_recv, own_send, own_sem, gain_send, gain_recv,
    x_send, x_recv, m_send, m_recv, ex_send, ex_recv, pair_send, pair_recv,
    o_send, o_recv, last_send, last_recv, x1_send, x1_recv,
):
    sec = lax.axis_index("section")
    row = lax.axis_index("row")
    col = lax.axis_index("col")
    other = 1 - sec
    cx, cy = col // SIDE, lax.rem(col, SIDE)
    odd = lax.rem(col, 2) == 1
    partner = jnp.where(odd, col - 1, col + 1)
    sibling = (other, row, col)
    up = (sec, lax.rem(row + jnp.where(sec == 0, 1, ROWS - 1), ROWS), col)
    down = (sec, lax.rem(row + jnp.where(sec == 0, ROWS - 1, 1), ROWS), col)
    xs = [cx] + [lax.rem(cx + d, SIDE) for d in range(1, SIDE)]
    ys = [cy] + [lax.rem(cy + d, SIDE) for d in range(1, SIDE)]
    along_x = [(sec, row, x * SIDE + cy) for x in xs]
    along_y = [(sec, row, cx * SIDE + y) for y in ys]
    ends = []

    def remote(src, dst, send, recv, device):
        return pltpu.make_async_remote_copy(
            src_ref=src, dst_ref=dst, send_sem=send, recv_sem=recv, device_id=device, device_id_type=MESH
        )

    def launch(src, dst, send, recv, device):
        copy = remote(src, dst, send, recv, device)
        copy.start()
        ends.append(copy)
        return copy

    def drain(keep=0):
        while len(ends) > keep:
            ends.pop(0).wait_send()

    def landed(place, recv):
        remote(place, place, gain_send, recv, sibling).wait_recv()

    tok_copy = pltpu.make_async_copy(tok_hbm, tok_ref, tok_sem)
    tok_copy.start()
    barrier = pltpu.get_barrier_semaphore()
    greeted = [sibling, up, down] + along_x[1:] + along_y[1:]
    for device in greeted:
        pl.semaphore_signal(barrier, 1, device_id=device, device_id_type=MESH)

    def slot_of(origin, i):
        return origin // 2, 2 * lax.rem(origin, 2) + i

    def half_of(x):
        return jnp.where(sec == 0, x[:, :HALF], x[:, HALF:])

    def prepare_stat(layer, x):
        square = x * x
        high = square.astype(BF)
        low = (square - high.astype(F32)).astype(BF)
        ones = jnp.ones((STAT, DH), BF)
        dims = (((1,), (1,)), ((), ()))
        line = lax.broadcasted_iota(jnp.int32, (STAT, DH), 0)
        for h in range(2):
            cols = slice(h * DH, (h + 1) * DH)
            total = lax.dot_general(ones, high[:, cols], dims, preferred_element_type=F32)
            total += lax.dot_general(ones, low[:, cols], dims, preferred_element_type=F32)
            top = total.astype(BF).astype(F32)
            rest = total - top
            rows = jnp.zeros((STAT, DH), F32)
            for n, part in enumerate((top[:, :DH], rest[:, :DH], top[:, DH:], rest[:, DH:])):
                rows = jnp.where(line == n, part, rows)
            xbuf[layer, h, cx, cy, TREE:] = rows.astype(BF)

    def prepare_mask():
        qpos = lax.broadcasted_iota(jnp.int32, (TREE, TREE), 0)
        kpos = lax.broadcasted_iota(jnp.int32, (TREE, TREE), 1)
        top, left = qpos < BLOCK, kpos < BLOCK
        live = jnp.where(
            top,
            jnp.where(left, live_ref[0, 0, 0], live_ref[0, 0, 1]),
            jnp.where(left, live_ref[0, 1, 0], live_ref[0, 1, 1]),
        )
        allowed = (kpos <= qpos) & (qpos <= last_ref[...]) & (live > 0)
        mask[...] = jnp.where(allowed, 1.0, 0.0).astype(F32)

    def before_barrier():
        prepare_mask()
        tok_copy.wait()
        prepare_stat(0, half_of(tok_ref[...]).astype(F32))

    def own_parts(half, kind):
        parts = []
        for i in range(2):
            sx, sy = slot_of(row, i)
            if kind == 0:
                base = pl.multiple_of(i * 512 + half * HALF, HALF)
                parts.append((wq_ref.at[pl.ds(base, HALF)], w_in.at[sec, sx, sy, :, pl.ds(0, 256)]))
                parts.append((wkv_ref.at[pl.ds(base, HALF)], w_in.at[sec, sx, sy, :, pl.ds(256, 128)]))
            else:
                base = pl.multiple_of(i * 256 + half * 128, 128)
                parts.append((wo_ref.at[pl.ds(base, 128)], w_out.at[sec, sx, sy]))
        return parts

    swaps, keeps = [], []
    n = 0
    for kind in range(2):
        for (src, dst), (mine, place) in zip(own_parts(other, kind), own_parts(sec, kind)):
            swaps.append((src, dst, own_send.at[n], own_sem.at[sec, n], sibling))
            keeps.append(pltpu.make_async_copy(mine, place, own_sem.at[sec, n]))
            n += 1
    for copy in keeps:
        copy.start()
    gains[sec] = jnp.broadcast_to(gain_ref[...].astype(F32), (8, 2 * HALF))
    before_barrier()
    pl.semaphore_wait(barrier, len(greeted))
    for swap in swaps[:4]:
        launch(*swap)
    launch(gains.at[sec], gains.at[sec], gain_send, gain_recv, sibling)
    for swap in swaps[4:]:
        launch(*swap)

    def wait_own(s, kind):
        for n in range(4) if kind == 0 else range(4, 6):
            sx, sy = slot_of(row, n // 2 if kind == 0 else n - 4)
            if kind == 0:
                place = w_in.at[s, sx, sy, :, pl.ds(0, 256) if n % 2 == 0 else pl.ds(256, 128)]
            else:
                place = w_out.at[s, sx, sy]
            pltpu.make_async_copy(place, place, own_sem.at[s, n]).wait()

    origins = {(0, 0): row, (0, 1): row}
    for d in range(1, 5):
        origins[d, 0] = lax.rem(row + jnp.where(sec == 0, ROWS - d, d), ROWS)
        origins[d, 1] = lax.rem(row + jnp.where(sec == 0, d, ROWS - d), ROWS)

    def chunk(s, kind, d, way, i):
        buf, send, recv = (w_in, wi_send, wi_recv) if kind == 0 else (w_out, wo_send, wo_recv)
        sx, sy = slot_of(origins[d, way], i // 2)
        rows = (HALF if kind == 0 else DH) // 2
        place = buf.at[s, sx, sy, pl.ds(i % 2 * rows, rows)]
        return place, send.at[s, way, d, i], recv.at[s, sx, sy, i % 2]

    def forward(s, kind, d, way, i):
        place, send, recv = chunk(s, kind, d, way, i)
        launch(place, place, send, recv, up if way == 0 else down)

    def start_ring(s, kind):
        wait_own(s, kind)
        for i in range(PARTS):
            for way in range(2):
                forward(s, kind, 0, way, i)

    def relay(s, kind, d, parts=range(PARTS)):
        for i in parts:
            for way in range(2):
                if d < 4 or i % 2 == way:
                    place, send, recv = chunk(s, kind, d, way, i)
                    landed(place, recv)
                    if d < 3 or (d == 3 and i % 2 == way):
                        forward(s, kind, d, way, i)

    X = (xbuf, x_send, x_recv)
    M = (mbuf, m_send, m_recv)

    def block_of(buf, recv, layer, h, along, across):
        x, y = (xs[across], ys[along]) if h == 0 else (xs[along], ys[across])
        return buf.at[layer, h, x, y], recv.at[layer, h, x, y]

    def phase_one(buf, send, recv, layer, halves=(0, 1)):
        for n, lines in ((SIDE, (along_y, along_x)), (0, (along_x, along_y))):
            for d in range(1, SIDE):
                for h in halves:
                    block, sem = block_of(buf, recv, layer, h, 0, 0)
                    launch(block, block, send.at[layer, h, n, d], sem, lines[h][d])

    def phase_two(buf, send, recv, layer, steps=(1, 3, 2)):
        for j in steps:
            for h in range(2):
                block, sem = block_of(buf, recv, layer, h, j, 0)
                landed(block, sem)
                for d in range(1, SIDE):
                    launch(block, block, send.at[layer, h, j, d], sem, (along_x, along_y)[h][d])

    def group_landed(buf, recv, layer, h, d):
        for j in range(SIDE):
            landed(*block_of(buf, recv, layer, h, j, d))

    def prepare_x(layer, x):
        scaled = (x * half_of(gains[layer])[0:1]).astype(BF)
        for h in range(2):
            xbuf[layer, h, cx, cy, :TREE] = scaled[:, h * DH:(h + 1) * DH]

    def add_stat(layer, blocks, first):
        lines = blocks[0][TREE:].astype(F32)
        for block in blocks[1:]:
            lines += block[TREE:].astype(F32)
        if first:
            stat[layer] = lines
        else:
            stat[layer] += lines

    def add_part(layer, part, first):
        for g in range(3):
            if first:
                acc[layer, g] = part[:, g * DH:(g + 1) * DH]
            else:
                acc[layer, g] += part[:, g * DH:(g + 1) * DH]

    def add_pair(layer, sx, sy, first=False):
        blocks = [xbuf[layer, h, sx, sy + i] for i in range(2) for h in range(2)]
        left = jnp.concatenate([block[:TREE] for block in blocks], axis=1)
        right = jnp.concatenate([w_in[layer, sx, sy + i] for i in range(2)], axis=0)
        add_stat(layer, blocks, first)
        add_part(layer, jnp.dot(left, right, preferred_element_type=F32), first)

    def exchange(layer):
        kv_bf[layer] = acc[layer, 2].astype(BF)
        launch(
            kv_bf.at[layer], ex_pair.at[layer, sec], pair_send.at[layer, 0], pair_recv.at[layer, 0], (sec, row, partner)
        )
        launch(acc.at[layer, 2], ex_kv.at[layer], ex_send.at[layer, 1], ex_recv.at[layer, 1], sibling)
        launch(stat.at[layer], ex_stat.at[layer], ex_send.at[layer, 2], ex_recv.at[layer, 2], sibling)
        launch(acc.at[layer, other], ex_q.at[layer], ex_send.at[layer, 0], ex_recv.at[layer, 0], sibling)

    def attend(layer):
        for n, place in enumerate((ex_q, ex_kv, ex_stat)):
            landed(place.at[layer], ex_recv.at[layer, n])
        lines = stat[layer] + ex_stat[layer]
        total = jnp.concatenate(
            [lines[2 * half:2 * half + 1] + lines[2 * half + 1:2 * half + 2] for half in range(2)], axis=1
        )
        inverse = lax.rsqrt(total * (1.0 / D) + EPSILON)
        inverse = jnp.transpose(jnp.broadcast_to(inverse, (DH, TREE)))
        query = ((acc[layer, sec] + ex_q[layer]) * inverse).astype(BF)
        mine = ((acc[layer, 2] + ex_kv[layer]) * inverse).astype(BF)
        place = ex_pair.at[layer, sec]
        landed(place, pair_recv.at[layer, 0])
        launch(place, place, pair_send.at[layer, 1], pair_recv.at[layer, 1], sibling)
        landed(ex_pair.at[layer, other], pair_recv.at[layer, 1])
        theirs = ((ex_pair[layer, 0].astype(F32) + ex_pair[layer, 1].astype(F32)) * inverse).astype(BF)
        keys = jnp.where(odd, theirs, mine)
        values = jnp.where(odd, mine, theirs)
        for h in range(2):
            seen = BLOCK * (h + 1)
            rows = slice(h * BLOCK, seen)
            scores = lax.dot_general(
                query[rows], keys[:seen], (((1,), (1,)), ((), ())), preferred_element_type=F32
            ) * DH ** (-0.5)
            scores = jnp.where(mask[rows, :seen] > 0.5, scores, F32(-1e30))
            weights = jnp.exp(scores - jnp.max(scores, axis=1, keepdims=True))
            probs = (weights / jnp.sum(weights, axis=1, keepdims=True)).astype(BF)
            mbuf[layer, h, cx, cy] = jnp.dot(probs, values[:seen], preferred_element_type=F32).astype(BF)
            phase_one(*M, layer, (h,))

    def project_pair(layer, sx, sy, first=False):
        rows = []
        for h in range(2):
            rows.append(jnp.concatenate([mbuf[layer, h, sx, sy + i] for i in range(2)], axis=1))
        right = jnp.concatenate([w_out[layer, sx, sy + i] for i in range(2)], axis=0)
        part = jnp.dot(jnp.concatenate(rows, axis=0), right, preferred_element_type=F32)
        for g in range(2):
            cols = slice(g * HALF, (g + 1) * HALF)
            if first:
                acc_o[layer, g] = part[:, cols]
            else:
                acc_o[layer, g] += part[:, cols]

    def all_landed(buf, recv, layer):
        for d in range(1, SIDE):
            for h in range(2):
                group_landed(buf, recv, layer, h, d)

    def near(work, layer, most=3, least=0):
        for d in range(least, most + 1):
            for way in range(2) if 0 < d < 4 else range(1):
                work(layer, *slot_of(origins[d, way], 0), d == 0)

    def flow(work, buf, recv, layer, steps=(0, 1, 3, 2)):
        for j in steps:
            for pair in range(0, SIDE, 2):
                for y in (pair, pair + 1):
                    if j:
                        landed(buf.at[layer, 0, xs[j], y], recv.at[layer, 0, xs[j], y])

                    @pl.when(cy != y)
                    def _():
                        landed(buf.at[layer, 1, xs[j], y], recv.at[layer, 1, xs[j], y])

                work(layer, xs[j], pair, j == 0 and pair == 0)

    start_ring(0, 0)
    landed(gains.at[other], gain_recv)
    prepare_x(0, half_of(tok_ref[...]).astype(F32))
    phase_one(*X, 0)
    relay(0, 0, 1)
    phase_two(*X, 0)
    relay(0, 0, 2)
    start_ring(0, 1)
    all_landed(xbuf, x_recv, 0)
    relay(0, 0, 3)
    near(add_pair, 0, 2)
    relay(0, 1, 1)
    start_ring(1, 0)
    near(add_pair, 0, 3, 3)
    relay(0, 0, 4)
    near(add_pair, 0, 4, 4)
    exchange(0)
    relay(0, 1, 2)
    attend(0)
    relay(0, 1, 3)
    relay(1, 0, 1)
    phase_two(*M, 0)
    relay(0, 1, 4)
    flow(project_pair, mbuf, m_recv, 0)
    launch(acc_o.at[0, other], ex_o, o_send, o_recv, sibling)
    landed(ex_o, o_recv)
    x1 = (half_of(tok_ref[...]).astype(F32) + (acc_o[0, sec] + ex_o[...])).astype(BF)
    x1buf[sec] = x1
    prepare_x(1, x1.astype(F32))
    prepare_stat(1, x1.astype(F32))
    phase_one(*X, 1)
    launch(x1buf.at[sec], x1buf.at[sec], x1_send, x1_recv, sibling)
    relay(1, 0, 2)
    phase_two(*X, 1)
    landed(x1buf.at[other], x1_recv)

    @pl.when(sec == 0)
    def _():
        for h in range(2):
            out_ref[0, :, h * HALF:(h + 1) * HALF] = x1buf[h]

    relay(1, 0, 3)
    start_ring(1, 1)
    relay(1, 0, 4)
    flow(add_pair, xbuf, x_recv, 1)
    exchange(1)
    relay(1, 1, 1)
    attend(1)
    relay(1, 1, 2)
    phase_two(*M, 1)
    relay(1, 1, 3)
    all_landed(mbuf, m_recv, 1)
    near(project_pair, 1)
    relay(1, 1, 4)
    near(project_pair, 1, 4, 4)
    last_copies = [
        remote(acc_o.at[1, h], ex_last.at[h], last_send.at[h], last_recv.at[h], (1, row, col)) for h in range(2)
    ]

    @pl.when(sec == 0)
    def _():
        for copy in last_copies:
            copy.start()

    drain()

    @pl.when(sec == 1)
    def _():
        for h in range(2):
            last_copies[h].wait_recv()
            x = x1buf[h].astype(F32)
            out_ref[0, :, h * HALF:(h + 1) * HALF] = (x + (acc_o[1, h] + ex_last[h])).astype(BF)

    @pl.when(sec == 0)
    def _():
        for copy in last_copies:
            copy.wait_send()


def shards(tokens, norm_gain, w_query, w_keyval, w_out, subtree_last, block_live):
    vmem = pl.BlockSpec(memory_space=pltpu.VMEM)
    hbm = pl.BlockSpec(memory_space=pltpu.HBM)
    dma = pltpu.SemaphoreType.DMA
    return pl.pallas_call(
        kernel,
        out_shape=pltpu.VMEM((1, TREE, 2 * HALF), BF),
        in_specs=[hbm, vmem, hbm, hbm, hbm, vmem, pl.BlockSpec(memory_space=pltpu.SMEM)],
        out_specs=vmem,
        scratch_shapes=[
            pltpu.VMEM((2, SIDE, SIDE, HALF, 3 * DH), BF),
            pltpu.VMEM((2, SIDE, SIDE, DH, 2 * HALF), BF),
            pltpu.VMEM((TREE, 2 * HALF), BF),
            pltpu.VMEM((2, 2, SIDE, SIDE, TREE + STAT, DH), BF),
            pltpu.VMEM((2, 2, SIDE, SIDE, BLOCK, DH), BF),
            pltpu.VMEM((2, 8, 2 * HALF), F32),
            pltpu.VMEM((2, 3, TREE, DH), F32),
            pltpu.VMEM((2, 2, TREE, HALF), F32),
            pltpu.VMEM((2, TREE, DH), F32),
            pltpu.VMEM((2, TREE, DH), F32),
            pltpu.VMEM((2, 2, TREE, DH), BF),
            pltpu.VMEM((2, TREE, DH), BF),
            pltpu.VMEM((2, STAT, DH), F32),
            pltpu.VMEM((2, STAT, DH), F32),
            pltpu.VMEM((TREE, HALF), F32),
            pltpu.VMEM((2, TREE, HALF), F32),
            pltpu.VMEM((2, TREE, HALF), BF),
            pltpu.VMEM((TREE, TREE), F32),
            dma,
            dma((2, 2, 4, PARTS)), dma((2, SIDE, SIDE, 2)), dma((2, 2, 4, PARTS)), dma((2, SIDE, SIDE, 2)),
            dma((6,)), dma((2, 6)), dma, dma,
            dma((2, 2, 5, SIDE)), dma((2, 2, SIDE, SIDE)), dma((2, 2, 5, SIDE)), dma((2, 2, SIDE, SIDE)),
            dma((2, 3)), dma((2, 3)), dma((2, 2)), dma((2, 2)),
            dma, dma, dma((2,)), dma((2,)), dma, dma,
        ],
        compiler_params=pltpu.CompilerParams(
            collective_id=0, has_side_effects=True, vmem_limit_bytes=60 << 20
        ),
    )(
        tokens, norm_gain, w_query[0], w_keyval[0], w_out[0],
        subtree_last.reshape(1, TREE), block_live,
    )


def solution(mesh):
    in_specs = (
        P("row", "col"),
        P("section", "col"),
        P("section", "row", "col"),
        P("section", "row", "col"),
        P("section", "row", "col"),
        P("row"),
        P("row", None, None),
    )
    out_specs = P("section", "row", "col")
    return jax.shard_map(shards, mesh=mesh, in_specs=in_specs, out_specs=out_specs, check_vma=False)
```
